256 devices in a mesh: band: 64 (over x, z, core), lev: 4 (over y).
Axes of the slice: x: 4, y: 4, z: 8, core: 2. Of those that a mesh axis runs over, the one named last changes fastest.
Arguments:
- jacobian: bfloat16 [20480, 13824], P('band', 'lev'), may hold values from -0.375 to 0.375
- departures: bfloat16 [20480, 256], P('band', 'lev'), may hold values from -6 to 6
- level_index: int32 [20480, 54], P('band'), may hold values from 0 to 134
- level_weight: bfloat16 [20480, 54], P('band'), may hold values from 0 to 1
- column_index: int32 [20480], P('band'), may hold values from 0 to 344063, as said below
- record_counts: int32 [4096], P('band'), may hold values from 0 to 5, as said below
Outputs:
- spectra: bfloat16 [136, 128, 2560], P('lev', None, 'band')
The draws below stay inside these ranges and needn't reach their ends.
Inputs may be any that keep to these rules, and one draw needn't show every extreme that they name: `column_index`: record i goes to band b = (i // 5) mod (number of bands) and its column lies in that band's rows: b * 2 * 2688 <= column < (b + 1) * 2 * 2688. `record_counts`: entry s * (number of bands) + b counts the live slots, the first ones, among the 5 slots that reader s fills for band b; in every draw some band receives 5 live records from every reader.
All inputs are finite; a program needn't handle non-finite values.
Results may differ from the reference program's by a relative error of at most 0.0055.
Values may be sent and summed in bfloat16 or wider, within the bound.
No kernel may reach another device: no remote copies, remote signals or barrier semaphores. Data moves between devices by JAX's collectives and lax.ppermute only.
A program may use at most 128 MiB of HBM per device.

```python
import math
import jax
import jax.numpy as jnp
from jax import lax

NCH = 256
KL = 54
LEVELS = 136
NLON = 2688
NM = 1280
ROWS = 2
CAP = 5
NLAT = 128
RECORDS = 20480
N_BAND = 64


def draw_record_counts(key, part):
    key_levels, key_counts, key_busiest = jax.random.split(jax.random.fold_in(key, 11), 3)
    levels_each = jax.random.randint(key_levels, (N_BAND,), 1, 5)
    ceiling = levels_each * CAP // 4 + 1
    counts = jax.random.randint(key_counts, (N_BAND, N_BAND), 0, ceiling[None, :])
    busiest = jax.random.randint(key_busiest, (), 0, N_BAND)
    owners = jnp.arange(N_BAND, dtype=jnp.int32)[None, :]
    counts = jnp.where(owners == busiest, CAP, counts)
    return counts.reshape(N_BAND * N_BAND).astype(jnp.int32)


def draw_column_index(key, part):
    record_total = N_BAND * N_BAND * CAP
    within = jax.random.randint(jax.random.fold_in(key, 23), (record_total,), 0, ROWS * NLON)
    owner = jnp.arange(record_total, dtype=jnp.int32) // CAP % N_BAND
    return (owner * (ROWS * NLON) + within).astype(jnp.int32)


def place_ends(array, own_key, low, top_value):
    dims = array.shape
    index_at = [jax.random.randint(jax.random.fold_in(own_key, axis), (), 0, dims[axis]) for axis in range(len(dims))]
    array = array.at[tuple(index_at)].set(low)
    longest = dims.index(max(dims))
    index_at[longest] = (index_at[longest] + 1) % dims[longest]
    return array.at[tuple(index_at)].set(top_value)


def level_of(stream_key, shape, cuts, low, top_value):
    level = 1.0
    for position, blocks in cuts:
        draws = jax.random.uniform(jax.random.fold_in(jax.random.fold_in(stream_key, 6), position), (blocks,), jnp.float32, low / len(cuts), top_value / len(cuts))
        level = level * jnp.repeat(jnp.exp(draws), shape[position] // blocks).reshape((-1,) + (1,) * (len(shape) - 1 - position))
    return level


def centred(stream_key, shape, spread, bound, cuts=(), kind=jnp.bfloat16):
    level = level_of(stream_key, shape, cuts, -0.22, 0.18) if cuts else 1.0
    array = jax.random.normal(stream_key, shape, jnp.float32) * spread * level
    return jnp.minimum(jnp.maximum(array, -bound), bound).astype(kind)


def setup_inputs(seed: int = 0) -> dict:
    key_list = jax.random.split(jax.random.key(seed), 7)
    return {
        "jacobian": centred(key_list[0], (RECORDS, NCH * KL), NCH ** -0.5, 0.375, ((0, 64), (1, 4))),
        "departures": centred(key_list[1], (RECORDS, NCH), 1.0, 6.0, ((0, 64), (1, 4))),
        "level_index": place_ends(jax.random.randint(key_list[2], (RECORDS, KL), 0, LEVELS - 1), jax.random.fold_in(key_list[2], 1), 0, (LEVELS - 1) - 1).astype(jnp.int32),
        "level_weight": jnp.clip(1.0 * jax.random.uniform(key_list[3], (RECORDS, KL), jnp.float32) ** level_of(key_list[3], (RECORDS, KL), ((0, 64),), -0.2, 0.2), 0.0, 1.0).astype(jnp.bfloat16),
        "column_index": draw_column_index(jax.random.fold_in(key_list[6], 71), 0),
        "record_counts": draw_record_counts(jax.random.fold_in(key_list[6], 71), 0),
    }


def dft_table():
    longitude = jnp.arange(NLON, dtype=jnp.int32)[:, None]
    wavenumber = jnp.arange(NM, dtype=jnp.int32)[None, :]
    phase_index = (longitude * wavenumber) % NLON
    angles = phase_index.astype(jnp.float32) * (2.0 * math.pi / NLON)
    stacked = jnp.stack([jnp.cos(angles), -jnp.sin(angles)], axis=2)
    return stacked.reshape(NLON, 2 * NM).astype(jnp.bfloat16)


def profiles(contrib, level_index, level_weight, record_total):
    weights = level_weight.astype(jnp.float32)
    row_offset = (jnp.arange(record_total, dtype=jnp.int32) * LEVELS)[:, None]
    lower_ids = (row_offset + level_index).reshape(-1)
    lower_terms = (contrib * (1.0 - weights)).reshape(-1)
    upper_terms = (contrib * weights).reshape(-1)
    summed = jax.ops.segment_sum(lower_terms, lower_ids, num_segments=record_total * LEVELS)
    summed = summed + jax.ops.segment_sum(upper_terms, lower_ids + 1, num_segments=record_total * LEVELS)
    return summed.reshape(record_total, LEVELS)


def contract_block(items):
    jacobian_block, departure_block = items
    return jnp.einsum("ock,oc->ok", jacobian_block.astype(jnp.float32), departure_block.astype(jnp.float32))


def reference(jacobian, departures, level_index, level_weight, column_index, record_counts):
    record_total = jacobian.shape[0]
    per_reader = record_total // N_BAND
    jacobian_blocks = jacobian.reshape(N_BAND, per_reader, NCH, KL)
    departure_blocks = departures.reshape(N_BAND, per_reader, NCH)
    contrib = lax.map(contract_block, (jacobian_blocks, departure_blocks)).reshape(record_total, KL)
    record_ids = jnp.arange(record_total, dtype=jnp.int32)
    usable = (record_ids % CAP) < record_counts[record_ids // CAP]
    contrib = jnp.where(usable[:, None], contrib, jnp.zeros_like(contrib))
    profile = profiles(contrib, level_index, level_weight, record_total)
    gridded = jnp.zeros((LEVELS, NLAT * NLON), jnp.float32).at[:, column_index].add(profile.T)
    increments = gridded.astype(jnp.bfloat16).reshape(LEVELS, NLAT, NLON)
    fourier = dft_table().astype(jnp.float32)

    def transform(level_rows):
        return jnp.dot(level_rows.astype(jnp.float32), fourier, precision=lax.Precision.HIGHEST).astype(jnp.bfloat16)

    return lax.map(transform, increments)
```

```python
import functools
import math

import jax
import jax.numpy as jnp
from jax import lax
from jax.experimental import pallas as pl
from jax.experimental.pallas import tpu as pltpu
from jax.sharding import PartitionSpec as P

KL = 54
KP = 56
LEVELS = 136
SHARE = 34
NLON = 2688
ROWS = 2
CAP = 5
CHANNELS = 64
WIDTH = CHANNELS * KL
RECS = 320
GROUP = 40
GROUPS = 8
ZS = 8
READERS = 64
CHUNKS = 22
LANES = 128
COEFS = 384
BLOCKS = 12
LOW = 32

F32 = jnp.float32
BF16 = jnp.bfloat16

SIN_TERMS = (
    math.pi,
    -(math.pi**3) / 6.0,
    math.pi**5 / 120.0,
    -(math.pi**7) / 5040.0,
    math.pi**9 / 362880.0,
)
MAGIC = 12582912.0


def dot_nt(a, b):
    return lax.dot_general(a, b, (((1,), (1,)), ((), ())), preferred_element_type=F32)


def dot_tn(a, b):
    return lax.dot_general(a, b, (((0,), (0,)), ((), ())), preferred_element_type=F32)


def lane_iota(shape):
    return lax.broadcasted_iota(jnp.int32, shape, 1)


def row_iota(shape):
    return lax.broadcasted_iota(jnp.int32, shape, 0)


def floor_div(values, divisor):
    return jnp.floor((values.astype(F32) + 0.5) * (1.0 / divisor))


def contract_kernel(jac_ref, dep_ref, out_ref):
    position = lane_iota((8, WIDTH))
    channel = floor_div(position, KL)
    level = position.astype(F32) - KL * channel
    spread = jnp.concatenate(
        [
            jnp.where(channel == (row_iota((8, WIDTH)) + 8 * t).astype(F32), 1.0, 0.0)
            for t in range(CHANNELS // 8)
        ],
        axis=0,
    ).astype(BF16)
    select = jnp.concatenate(
        [
            jnp.where(level == (row_iota((8, WIDTH)) + 8 * t).astype(F32), 1.0, 0.0)
            for t in range(KP // 8)
        ],
        axis=0,
    ).astype(BF16)
    for start, size in ((0, 128), (128, 128), (256, 64)):
        rows = slice(start, start + size)
        wide = jnp.dot(dep_ref[rows, :], spread, preferred_element_type=F32)
        product = jac_ref[rows, :].astype(F32) * wide
        high = product.astype(BF16)
        low = (product - high.astype(F32)).astype(BF16)
        out_ref[:, rows] = dot_nt(select, high) + dot_nt(select, low)


def prepare_kernel(index_ref, weight_ref, column_ref, count_ref, place_ref, aux_ref):
    eye = jnp.where(row_iota((KP, KL)) == lane_iota((KP, KL)), 1.0, 0.0).astype(BF16)
    place_ref[...] = dot_nt(eye, index_ref[...].astype(F32).astype(BF16)) + dot_nt(
        eye, weight_ref[...]
    )
    lanes = lane_iota((8, RECS))
    band = floor_div(lanes, CAP)
    slot = lanes.astype(F32) - CAP * band
    repeat = jnp.where(
        floor_div(lane_iota((READERS, RECS)), CAP) == row_iota((READERS, RECS)).astype(F32),
        1.0,
        0.0,
    ).astype(BF16)
    counts = jnp.broadcast_to(count_ref[...].astype(F32), (8, READERS)).astype(BF16)
    counts = jnp.dot(counts, repeat, preferred_element_type=F32)
    live = jnp.where(slot < counts, 1.0, 0.0)
    column = jnp.broadcast_to(column_ref[...], (8, RECS)) - band.astype(jnp.int32) * (ROWS * NLON)
    high = lax.shift_right_logical(column, 5)
    low = column - high * LOW
    which = row_iota((8, RECS))
    aux_ref[...] = jnp.where(
        which == 0, live, jnp.where(which == 2, high.astype(F32), low.astype(F32))
    )


def pack_kernel(own_ref, one_ref, two_ref, three_ref, place_ref, aux_ref, out_ref, sum_ref):
    sum_ref[...] = (own_ref[...] + one_ref[...]) + (two_ref[...] + three_ref[...])
    first = lax.axis_index("lev") * SHARE
    live = aux_ref[0:1, :]
    blocks = []
    for start, size in ((0, 16), (16, 16), (32, 8)):
        target = (row_iota((size, RECS)) + (first + start)).astype(F32)
        total = jnp.zeros((size, RECS), F32)
        for k in range(KL):
            hat = jnp.maximum(1.0 - jnp.abs(target - place_ref[k : k + 1, :]), 0.0)
            total = total + hat * sum_ref[k : k + 1, :]
        blocks.append(total * live)
    which = row_iota((8, RECS))
    last = jnp.where(which < 2, blocks[2], jnp.where(which < 4, aux_ref[...], 0.0))
    blocks[2] = jnp.concatenate([last, jnp.zeros((8, RECS), F32)], axis=0)
    padding = jnp.zeros((16, COEFS - RECS), F32)
    blocks = [jnp.concatenate([block, padding], axis=1) for block in blocks]
    lanes = lane_iota((16, LANES))
    for g in range(GROUPS):
        parts = [
            pltpu.roll(block, (GROUP * (t - g)) % COEFS, 1)[:, :LANES]
            for t, block in enumerate(blocks)
        ]
        message = jnp.where(
            lanes < GROUP,
            parts[0],
            jnp.where(
                lanes < 2 * GROUP, parts[1], jnp.where(lanes < 3 * GROUP, parts[2], 0.0)
            ),
        ).astype(BF16)
        for z in range(ZS):
            out_ref[(g // 2) * 16 + z * 2 + g % 2] = message


def transform_kernel(in_ref, out_ref, block_ref, acc_ref):
    z = lax.rem(lax.axis_index("band") // 2, ZS)
    lanes = lane_iota((16, LANES))
    lane = lane_iota((8, COEFS))
    tile = lane // LANES
    inside = lane - tile * LANES
    slot = floor_div(inside, GROUP).astype(jnp.int32)
    within = inside - slot * GROUP
    owner = tile * 3 + slot
    wave = (owner // 2) * 320 + (owner % 2) * 20 + z * 40 + within // 2
    wave = jnp.minimum(wave, 1279)
    odd = (within % 2).astype(F32)
    residue = wave.astype(F32) - 84.0 * floor_div(wave, 84)
    upper = (wave // 64) * 64
    which = row_iota((8, COEFS))
    factors = jnp.where(
        which == 0,
        residue * LOW,
        jnp.where(
            which == 1,
            upper.astype(F32),
            jnp.where(
                which == 2,
                (wave - upper).astype(F32),
                jnp.where(which == 3, odd * (NLON // 4), 0.0),
            ),
        ),
    ).astype(BF16)
    acc_ref[...] = jnp.zeros_like(acc_ref)
    band2 = floor_div(lanes - floor_div(lanes, GROUP).astype(jnp.int32) * GROUP, CAP) * 2.0
    step_rows = row_iota((16, LANES)).astype(F32)

    for v in range(CHUNKS):
        messages = [
            in_ref[3 * v + s].astype(F32) if 3 * v + s < READERS else jnp.zeros((16, LANES), F32)
            for s in range(3)
        ]
        for t in range(3):
            parts = [pltpu.roll(messages[s], (GROUP * (s - t)) % LANES, 1) for s in range(3)]
            block_ref[t] = jnp.where(
                lanes < GROUP,
                parts[0],
                jnp.where(
                    lanes < 2 * GROUP, parts[1], jnp.where(lanes < 3 * GROUP, parts[2], 0.0)
                ),
            )
        high = block_ref[2, 2:3, :]
        low = block_ref[2, 3:4, :]
        which = row_iota((8, LANES))
        numbers = jnp.where(
            which == 0,
            jnp.broadcast_to(high, (8, LANES)),
            jnp.where(
                which < 3,
                jnp.broadcast_to(low, (8, LANES)),
                jnp.where(which == 3, 1.0, 0.0),
            ),
        ).astype(BF16)
        turns = dot_tn(numbers, factors) * (1.0 / NLON)
        turns = turns - ((turns + MAGIC) - MAGIC)
        square = turns * turns
        series = SIN_TERMS[4]
        for term in SIN_TERMS[3::-1]:
            series = series * square + term
        sine = series * turns
        table = (1.0 - 2.0 * (sine * sine)).astype(BF16)
        row = band2 + jnp.where(jnp.broadcast_to(high, (16, LANES)) >= 84.0, 1.0, 0.0)
        mask = jnp.where(row == step_rows, 1.0, 0.0)
        left = jnp.concatenate(
            [
                (mask * jnp.broadcast_to(block_ref[n // 16, n % 16 : n % 16 + 1, :], (16, LANES)))
                for n in range(SHARE)
            ],
            axis=0,
        ).astype(BF16)
        acc_ref[...] += jnp.dot(left, table, preferred_element_type=F32)

    for d in range(GROUPS):
        tile, slot = d // 3, d % 3
        for i in range(BLOCKS):
            parts = [
                pltpu.roll(
                    acc_ref[
                        pl.ds((t * BLOCKS + i) * 16, 16), LANES * tile : LANES * (tile + 1)
                    ],
                    (GROUP * (t - slot)) % LANES,
                    1,
                )
                if t * BLOCKS + i < SHARE
                else jnp.zeros((16, LANES), F32)
                for t in range(3)
            ]
            out_ref[d, i] = jnp.where(
                lanes < GROUP, parts[0], jnp.where(lanes < 2 * GROUP, parts[1], parts[2])
            ).astype(BF16)


def place_kernel(in_ref, out_ref):
    for i in range(BLOCKS):
        for g in range(GROUPS):
            values = in_ref[g, i].astype(F32)
            for t in range(3):
                if t * BLOCKS + i < SHARE:
                    moved = pltpu.roll(values, (-GROUP * t) % LANES, 1) if t else values
                    out_ref[t * BLOCKS + i, 16 * g : 16 * g + 16, :] = moved[:, :GROUP].astype(BF16)


def call(kernel, out_shape, scratch=(), **keywords):
    return pl.pallas_call(
        kernel,
        out_shape=out_shape,
        scratch_shapes=list(scratch),
        compiler_params=pltpu.CompilerParams(vmem_limit_bytes=32 * 1024 * 1024),
        **keywords,
    )


def local(jacobian, departures, level_index, level_weight, column_index, record_counts):
    partial = call(contract_kernel, jax.ShapeDtypeStruct((KP, RECS), F32))(jacobian, departures)
    others = [
        lax.ppermute(partial, "lev", [(i, (i + k) % 4) for i in range(4)]) for k in (2, 1, 3)
    ]
    place, aux = call(
        prepare_kernel,
        (jax.ShapeDtypeStruct((KP, RECS), F32), jax.ShapeDtypeStruct((8, RECS), F32)),
    )(level_index, level_weight, column_index.reshape(1, RECS), record_counts.reshape(1, READERS))
    packed = call(
        pack_kernel,
        jax.ShapeDtypeStruct((READERS, 16, LANES), BF16),
        [pltpu.VMEM((KP, RECS), F32)],
    )(partial, *others, place, aux)
    arrived = lax.all_to_all(packed, "band", split_axis=0, concat_axis=0, tiled=True)
    spectra = call(
        transform_kernel,
        jax.ShapeDtypeStruct((GROUPS, BLOCKS, 16, LANES), BF16),
        [pltpu.VMEM((3, 16, LANES), F32), pltpu.VMEM((SHARE * 16, COEFS), F32)],
    )(arrived)
    groups = [[x * 16 + z * 2 + c for x in range(4) for c in range(2)] for z in range(ZS)]
    spectra = lax.all_to_all(
        spectra, "band", split_axis=0, concat_axis=0, axis_index_groups=groups, tiled=True
    )
    return call(place_kernel, jax.ShapeDtypeStruct((SHARE, 128, GROUP), BF16))(spectra)


def solution(mesh):
    placed = (
        P("band", "lev"),
        P("band", "lev"),
        P("band", None),
        P("band", None),
        P("band"),
        P("band"),
    )
    return jax.shard_map(
        local, mesh=mesh, in_specs=placed, out_specs=P("lev", None, "band"), check_vma=False
    )
```

```python
import math

import jax
import jax.numpy as jnp
from jax import lax
from jax.experimental import pallas as pl
from jax.experimental.pallas import tpu as pltpu
from jax.sharding import PartitionSpec as P

KL = 54
KP = 56
SHARE = 34
NLON = 2688
ROWS = 2
CAP = 5
CHANNELS = 64
WIDTH = CHANNELS * KL
RECS = 320
PIECES = ((0, 128), (128, 128), (256, 64))
GROUP = 40
GROUPS = 8
XS = 4
ZS = 8
CORES = 2
BANDS = 64
SENDERS = XS * ZS
TILES = 11
LANES = 128
DEPTH = CORES * TILES * LANES
COEFS = 40
PARTS = 5
TOGETHER = 8
LOW = 32

F32 = jnp.float32
BF16 = jnp.bfloat16

SIN_TERMS = (
    math.pi,
    -(math.pi**3) / 6.0,
    math.pi**5 / 120.0,
    -(math.pi**7) / 5040.0,
    math.pi**9 / 362880.0,
)
MAGIC = 12582912.0


def dot_nt(a, b):
    return lax.dot_general(a, b, (((1,), (1,)), ((), ())), preferred_element_type=F32)


def dot_tn(a, b):
    return lax.dot_general(a, b, (((0,), (0,)), ((), ())), preferred_element_type=F32)


def lane_iota(shape):
    return lax.broadcasted_iota(jnp.int32, shape, 1)


def row_iota(shape):
    return lax.broadcasted_iota(jnp.int32, shape, 0)


def floor_div(values, divisor):
    return jnp.floor((values.astype(F32) + 0.5) * (1.0 / divisor))


def contract_kernel(jac_hbm, dep_ref, out_ref, jac_ref, wide_ref, semaphores):
    copies = [
        pltpu.make_async_copy(
            jac_hbm.at[pl.ds(start, size)], jac_ref.at[pl.ds(start, size)], semaphores.at[p]
        )
        for p, (start, size) in enumerate(PIECES)
    ]
    for copy in copies:
        copy.start()
    position = lane_iota((8, WIDTH))
    channel = floor_div(position, KL)
    level = position.astype(F32) - KL * channel
    spread = jnp.concatenate(
        [
            jnp.where(channel == (row_iota((8, WIDTH)) + 8 * t).astype(F32), 1.0, 0.0)
            for t in range(CHANNELS // 8)
        ],
        axis=0,
    ).astype(BF16)
    select = jnp.concatenate(
        [
            jnp.where(level == (row_iota((8, WIDTH)) + 8 * t).astype(F32), 1.0, 0.0)
            for t in range(KP // 8)
        ],
        axis=0,
    ).astype(BF16)
    wide_ref[...] = dot_tn(dep_ref[...], spread)
    for copy, (start, size) in zip(copies, PIECES):
        records = slice(start, start + size)
        copy.wait()
        product = jac_ref[records, :].astype(F32) * wide_ref[records, :]
        high = product.astype(BF16)
        low = (product - high.astype(F32)).astype(BF16)
        out_ref[:, records] = dot_nt(select, high) + dot_nt(select, low)


def prepare_kernel(index_ref, weight_ref, column_ref, count_ref, place_ref, aux_ref):
    place_ref[...] = index_ref[...].astype(F32) + weight_ref[...].astype(F32)
    lanes = lane_iota((8, RECS))
    band = floor_div(lanes, CAP)
    slot = lanes.astype(F32) - CAP * band
    repeat = jnp.where(
        floor_div(lane_iota((BANDS, RECS)), CAP) == row_iota((BANDS, RECS)).astype(F32),
        1.0,
        0.0,
    ).astype(BF16)
    counts = jnp.broadcast_to(count_ref[...].astype(F32), (8, BANDS)).astype(BF16)
    counts = jnp.dot(counts, repeat, preferred_element_type=F32)
    live = jnp.where(slot < counts, 1.0, 0.0)
    column = jnp.broadcast_to(column_ref[...], (8, RECS)) - band.astype(jnp.int32) * (ROWS * NLON)
    high = lax.shift_right_logical(column, 5)
    low = column - high * LOW
    which = row_iota((8, RECS))
    aux_ref[...] = jnp.where(
        which == 0, live, jnp.where(which == 2, high.astype(F32), low.astype(F32))
    )


def pack_kernel(own_ref, one_ref, two_ref, three_ref, place_ref, aux_ref, out_ref, sum_ref):
    sum_ref[...] = (own_ref[...] + one_ref[...]) + (two_ref[...] + three_ref[...])
    first = lax.axis_index("lev") * SHARE
    live = aux_ref[0:1, :]
    blocks = []
    for start, size in ((0, 24), (24, 8), (32, 8)):
        target = (row_iota((size, RECS)) + (first + start)).astype(F32)
        total = jnp.zeros((size, RECS), F32)
        for k in range(KL):
            hat = jnp.maximum(1.0 - jnp.abs(target - place_ref[k : k + 1, :]), 0.0)
            total = total + hat * sum_ref[k : k + 1, :]
        blocks.append(total * live)
    which = row_iota((8, RECS))
    blocks[2] = jnp.where(which < 2, blocks[2], jnp.where(which < 4, aux_ref[...], 0.0))
    full = 3 * LANES
    upper, middle, last = [
        jnp.concatenate([block, jnp.zeros((block.shape[0], full - RECS), F32)], axis=1)
        for block in blocks
    ]

    def moved(block, source, target):
        return pltpu.roll(block, (target - source) % full, 1)[:, :LANES]

    lanes = lane_iota((24, LANES))
    low_rows = row_iota((8, LANES)) < 4
    for x in range(XS):
        one, two, spot = 2 * GROUP * x, 2 * GROUP * x + GROUP, 2 * GROUP
        rest = jnp.concatenate(
            [
                moved(middle, one, spot),
                moved(middle, two, spot),
                jnp.where(low_rows, moved(last, one, spot), pltpu.roll(moved(last, two, spot), 4, 0)),
            ],
            axis=0,
        )
        message = jnp.where(
            lanes < spot, moved(upper, one, 0), jnp.where(lanes < 3 * GROUP, rest, 0.0)
        ).astype(BF16)
        for z in range(ZS):
            out_ref[x * ZS + z] = message


def wave_factors(x, z, core):
    shape = (88, LANES)
    row = row_iota(shape)
    lane = lane_iota(shape)
    target = jnp.bitwise_and(row + x, 3)
    first = target * 320 + (core * 20 + z * 40)
    inner = jnp.maximum(jnp.where(row < 48, row - 8, row - 48), 0)
    step = lax.shift_right_logical(inner, 1)
    odd = inner - 2 * step
    wave = jnp.where(row < 8, first, step)
    quarter = jnp.where(
        row < 4, 0, jnp.where(row < 8, -1, jnp.where(row < 48, odd, odd - 1))
    ).astype(F32)
    residue = wave.astype(F32) - 84.0 * floor_div(wave, 84)
    lower = jnp.bitwise_and(wave, 63)
    values = jnp.where(
        lane == 0,
        residue * LOW,
        jnp.where(
            lane == 1,
            (wave - lower).astype(F32),
            jnp.where(
                lane == 2,
                lower.astype(F32),
                jnp.where(lane == 3, quarter * (NLON // 4), 0.0),
            ),
        ),
    )
    return values[:, :16].astype(BF16)


def transform_kernel(
    own_ref, other_ref, out0_ref, out1_ref, out2_ref, out3_ref, block_ref, left_ref, table_ref
):
    outs = (out0_ref, out1_ref, out2_ref, out3_ref)
    place = lax.axis_index("band")
    factors = wave_factors(place // 16, lax.rem(place // 2, ZS), lax.rem(place, 2))
    lanes8 = lane_iota((8, LANES))
    lanes = lane_iota((16, LANES))
    slot = floor_div(lanes, GROUP)
    band2 = floor_div(lanes.astype(F32) - GROUP * slot, CAP) * 2.0
    step_rows = row_iota((16, LANES)).astype(F32)
    which = row_iota((16, LANES))
    for c in range(CORES):
        left_ref[c, SHARE * 16 :, :] = jnp.zeros((PARTS * LANES - SHARE * 16, DEPTH), BF16)

    for v in range(CORES * TILES):
        half, tile = v // TILES, v % TILES
        arrived = (own_ref, other_ref)[half]
        columns = slice(LANES * v, LANES * (v + 1))
        messages = [
            arrived[3 * tile + s].astype(F32)
            if 3 * tile + s < SENDERS
            else jnp.zeros((24, LANES), F32)
            for s in range(3)
        ]
        for c in range(CORES):
            groups = []
            for s, message in enumerate(messages):
                near = (GROUP * (s - c)) % LANES
                far = (GROUP * (s - 2)) % LANES
                last = pltpu.roll(message[16:24], far, 1)
                groups.append(
                    [pltpu.roll(message[8 * t : 8 * t + 8], near, 1) for t in range(3)]
                    + [
                        pltpu.roll(message[8 * c : 8 * c + 8], far, 1),
                        pltpu.roll(last, 4, 0) if c else last,
                    ]
                )
            for t in range(5):
                block_ref[v, c, t] = jnp.where(
                    lanes8 < GROUP,
                    groups[0][t],
                    jnp.where(
                        lanes8 < 2 * GROUP,
                        groups[1][t],
                        jnp.where(lanes8 < 3 * GROUP, groups[2][t], 0.0),
                    ),
                )
            high = jnp.broadcast_to(block_ref[v, c, 4, 2:3, :], (16, LANES))
            low = jnp.broadcast_to(block_ref[v, c, 4, 3:4, :], (16, LANES))
            numbers = jnp.where(
                which == 0, high, jnp.where(which < 3, low, jnp.where(which == 3, 1.0, 0.0))
            ).astype(BF16)
            turns = jnp.dot(factors, numbers, preferred_element_type=F32) * (1.0 / NLON)
            turns = turns - ((turns + MAGIC) - MAGIC)
            square = turns * turns
            series = SIN_TERMS[4]
            for term in SIN_TERMS[3::-1]:
                series = series * square + term
            sine = series * turns
            waves = 1.0 - 2.0 * (sine * sine)
            inner_cosine, inner_sine = waves[8:48], waves[48:88]
            for pair in range(2):
                table_ref[c, 80 * pair : 80 * pair + 80, columns] = jnp.concatenate(
                    [
                        waves[d : d + 1] * inner_cosine - waves[4 + d : 5 + d] * inner_sine
                        for d in (2 * pair, 2 * pair + 1)
                    ],
                    axis=0,
                ).astype(BF16)
            row = band2 + jnp.where(high >= 84.0, 1.0, 0.0)
            mask = jnp.where(row == step_rows, 1.0, 0.0)
            for n in range(SHARE):
                left_ref[c, 16 * n : 16 * n + 16, columns] = (
                    mask * block_ref[v, c, n // 8, n % 8 : n % 8 + 1, :]
                ).astype(BF16)

    for c in range(CORES):
        for start, size in ((0, 256), (256, 256), (512, 128)):
            result = dot_nt(table_ref[c], left_ref[c, start : start + size, :])
            for part in range(size // LANES):
                for k in range(XS):
                    group = (2 * (-k % XS) + c) % GROUPS
                    piece = result[
                        COEFS * k : COEFS * (k + 1), LANES * part : LANES * (part + 1)
                    ]
                    if group:
                        piece = pltpu.roll(piece, 16 * group, 1)
                    outs[k][c, start // LANES + part] = piece.astype(BF16)


def place_kernel(zero_ref, one_ref, two_ref, three_ref, out_hbm, out_ref, semaphores):
    shift = 32 * (lax.axis_index("band") // 16)
    slot = lax.shift_right_logical(lane_iota((COEFS, LANES)), 4)
    sources = (zero_ref, three_ref, two_ref, one_ref)
    copies = []
    for part in range(PARTS):
        values = [sources[g // 2][g % 2, part].astype(F32) for g in range(GROUPS)]
        first = part * TOGETHER
        count = min(TOGETHER, SHARE - first)
        for q in range(count):
            merged = values[(-q) % TOGETHER]
            for p in range(1, TOGETHER):
                merged = jnp.where(slot == p, values[(p - q) % TOGETHER], merged)
            turn = lax.rem(shift + (LANES - 16 * q), LANES)
            out_ref[first + q] = pltpu.roll(merged, turn, 1).astype(BF16)
        copy = pltpu.make_async_copy(
            out_ref.at[pl.ds(first, count)], out_hbm.at[pl.ds(first, count)], semaphores.at[part]
        )
        copy.start()
        copies.append(copy)
    for copy in copies:
        copy.wait()


def call(kernel, out_shape, scratch=(), limit=32, **keywords):
    return pl.pallas_call(
        kernel,
        out_shape=out_shape,
        scratch_shapes=list(scratch),
        compiler_params=pltpu.CompilerParams(vmem_limit_bytes=limit * 1024 * 1024),
        **keywords,
    )


def x_shift(k):
    return [
        (x * 16 + rest, (x + k) % XS * 16 + rest) for x in range(XS) for rest in range(ZS * CORES)
    ]


def local(jacobian, departures, level_index, level_weight, column_index, record_counts):
    vmem = pl.BlockSpec(memory_space=pltpu.VMEM)
    hbm = pl.BlockSpec(memory_space=pltpu.HBM)
    partial = call(
        contract_kernel,
        jax.ShapeDtypeStruct((KP, RECS), F32),
        [
            pltpu.VMEM((RECS, WIDTH), BF16),
            pltpu.VMEM((RECS, WIDTH), F32),
            pltpu.SemaphoreType.DMA((len(PIECES),)),
        ],
        limit=59,
        in_specs=[hbm, vmem],
        out_specs=vmem,
    )(jacobian, departures.T)
    others = [
        lax.ppermute(partial, "lev", [(i, (i + k) % 4) for i in range(4)]) for k in (2, 1, 3)
    ]
    place, aux = call(
        prepare_kernel,
        (jax.ShapeDtypeStruct((KL, RECS), F32), jax.ShapeDtypeStruct((8, RECS), F32)),
    )(level_index.T, level_weight.T, column_index.reshape(1, RECS), record_counts.reshape(1, BANDS))
    packed = call(
        pack_kernel,
        jax.ShapeDtypeStruct((SENDERS, 24, LANES), BF16),
        [pltpu.VMEM((KP, RECS), F32)],
    )(partial, *others, place, aux)
    same_core = [
        [x * 16 + z * 2 + c for x in range(XS) for z in range(ZS)] for c in range(CORES)
    ]
    arrived = lax.all_to_all(
        packed, "band", split_axis=0, concat_axis=0, axis_index_groups=same_core, tiled=True
    )
    other = lax.ppermute(arrived, "band", [(i, i ^ 1) for i in range(BANDS)])
    spectra = call(
        transform_kernel,
        [jax.ShapeDtypeStruct((CORES, PARTS, COEFS, LANES), BF16)] * XS,
        [
            pltpu.VMEM((CORES * TILES, CORES, 5, 8, LANES), F32),
            pltpu.VMEM((CORES, PARTS * LANES, DEPTH), BF16),
            pltpu.VMEM((CORES, XS * COEFS, DEPTH), BF16),
        ],
    )(arrived, other)
    received = [spectra[0]] + [None] * 3
    for k in (2, 1, 3):
        received[k] = lax.ppermute(spectra[k], "band", x_shift(k))
    placed = call(
        place_kernel,
        jax.ShapeDtypeStruct((SHARE, COEFS, LANES), BF16),
        [pltpu.VMEM((SHARE, COEFS, LANES), BF16), pltpu.SemaphoreType.DMA((PARTS,))],
        in_specs=[vmem] * 4,
        out_specs=hbm,
    )(*received)
    return jnp.transpose(placed, (0, 2, 1))


def solution(mesh):
    placed = (
        P("band", "lev"),
        P("band", "lev"),
        P("band", None),
        P("band", None),
        P("band"),
        P("band"),
    )
    return jax.shard_map(
        local, mesh=mesh, in_specs=placed, out_specs=P("lev", None, "band"), check_vma=False
    )
```

```python
import math

import jax
import jax.numpy as jnp
from jax import lax
from jax.experimental import pallas as pl
from jax.experimental.pallas import tpu as pltpu
from jax.sharding import PartitionSpec as P

KL = 54
KP = 56
SHARE = 34
NLON = 2688
ROWS = 2
CAP = 5
CHANNELS = 64
WIDTH = CHANNELS * KL
RECS = 320
PIECES = ((0, 128), (128, 128), (256, 64))
GROUP = 40
GROUPS = 8
XS = 4
ZS = 8
CORES = 2
BANDS = 64
SENDERS = XS * ZS
TILES = 11
LANES = 128
DEPTH = TILES * LANES
COEFS = 40
PARTS = 5
TOGETHER = 8
LOW = 32

F32 = jnp.float32
BF16 = jnp.bfloat16

SIN_TERMS = (
    math.pi,
    -(math.pi**3) / 6.0,
    math.pi**5 / 120.0,
    -(math.pi**7) / 5040.0,
    math.pi**9 / 362880.0,
)
MAGIC = 12582912.0


def dot_nt(a, b):
    return lax.dot_general(a, b, (((1,), (1,)), ((), ())), preferred_element_type=F32)


def dot_tn(a, b):
    return lax.dot_general(a, b, (((0,), (0,)), ((), ())), preferred_element_type=F32)


def lane_iota(shape):
    return lax.broadcasted_iota(jnp.int32, shape, 1)


def row_iota(shape):
    return lax.broadcasted_iota(jnp.int32, shape, 0)


def floor_div(values, divisor):
    return jnp.floor((values.astype(F32) + 0.5) * (1.0 / divisor))


def contract_kernel(jac_hbm, dep_hbm, out_ref, jac_ref, dep_ref, wide_ref, semaphores):
    departures = pltpu.make_async_copy(dep_hbm, dep_ref, semaphores.at[len(PIECES)])
    departures.start()
    copies = [
        pltpu.make_async_copy(
            jac_hbm.at[pl.ds(start, size)], jac_ref.at[pl.ds(start, size)], semaphores.at[p]
        )
        for p, (start, size) in enumerate(PIECES)
    ]
    for copy in copies:
        copy.start()
    position = lane_iota((8, WIDTH))
    channel = floor_div(position, KL)
    level = position.astype(F32) - KL * channel
    spread = jnp.concatenate(
        [
            jnp.where(channel == (row_iota((8, WIDTH)) + 8 * t).astype(F32), 1.0, 0.0)
            for t in range(CHANNELS // 8)
        ],
        axis=0,
    ).astype(BF16)
    select = jnp.concatenate(
        [
            jnp.where(level == (row_iota((8, WIDTH)) + 8 * t).astype(F32), 1.0, 0.0)
            for t in range(KP // 8)
        ],
        axis=0,
    ).astype(BF16)
    departures.wait()
    wide_ref[...] = dot_tn(dep_ref[...], spread)
    for copy, (start, size) in zip(copies, PIECES):
        records = slice(start, start + size)
        copy.wait()
        product = jac_ref[records, :].astype(F32) * wide_ref[records, :]
        high = product.astype(BF16)
        low = (product - high.astype(F32)).astype(BF16)
        out_ref[:, records] = dot_nt(select, high) + dot_nt(select, low)


def prepare_kernel(index_ref, weight_ref, column_ref, count_ref, place_ref, aux_ref):
    place_ref[...] = index_ref[...].astype(F32) + weight_ref[...].astype(F32)
    lanes = lane_iota((8, RECS))
    band = floor_div(lanes, CAP)
    slot = lanes.astype(F32) - CAP * band
    repeat = jnp.where(
        floor_div(lane_iota((BANDS, RECS)), CAP) == row_iota((BANDS, RECS)).astype(F32),
        1.0,
        0.0,
    ).astype(BF16)
    counts = jnp.broadcast_to(count_ref[...].astype(F32), (8, BANDS)).astype(BF16)
    counts = jnp.dot(counts, repeat, preferred_element_type=F32)
    live = jnp.where(slot < counts, 1.0, 0.0)
    column = jnp.broadcast_to(column_ref[...], (8, RECS)) - band.astype(jnp.int32) * (ROWS * NLON)
    high = lax.shift_right_logical(column, 5)
    low = column - high * LOW
    which = row_iota((8, RECS))
    aux_ref[...] = jnp.where(
        which == 0, live, jnp.where(which == 2, high.astype(F32), low.astype(F32))
    )


def pack_kernel(own_ref, one_ref, two_ref, three_ref, place_ref, aux_ref, out_ref, sum_ref):
    sum_ref[...] = (own_ref[...] + one_ref[...]) + (two_ref[...] + three_ref[...])
    first = lax.axis_index("lev") * SHARE
    live = aux_ref[0:1, :]
    blocks = []
    for start, size in ((0, 24), (24, 8), (32, 8)):
        target = (row_iota((size, RECS)) + (first + start)).astype(F32)
        total = jnp.zeros((size, RECS), F32)
        for k in range(KL):
            hat = jnp.maximum(1.0 - jnp.abs(target - place_ref[k : k + 1, :]), 0.0)
            total = total + hat * sum_ref[k : k + 1, :]
        blocks.append(total * live)
    which = row_iota((8, RECS))
    blocks[2] = jnp.where(which < 2, blocks[2], jnp.where(which < 4, aux_ref[...], 0.0))
    full = 3 * LANES
    upper, middle, last = [
        jnp.concatenate([block, jnp.zeros((block.shape[0], full - RECS), F32)], axis=1)
        for block in blocks
    ]

    def moved(block, source, target):
        return pltpu.roll(block, (target - source) % full, 1)[:, :LANES]

    lanes = lane_iota((24, LANES))
    low_rows = row_iota((8, LANES)) < 4
    for x in range(XS):
        one, two, spot = 2 * GROUP * x, 2 * GROUP * x + GROUP, 2 * GROUP
        rest = jnp.concatenate(
            [
                moved(middle, one, spot),
                moved(middle, two, spot),
                jnp.where(low_rows, moved(last, one, spot), pltpu.roll(moved(last, two, spot), 4, 0)),
            ],
            axis=0,
        )
        message = jnp.where(
            lanes < spot, moved(upper, one, 0), jnp.where(lanes < 3 * GROUP, rest, 0.0)
        ).astype(BF16)
        for z in range(ZS):
            out_ref[x * ZS + z] = message


def wave_factors(x, z, core):
    shape = (48, LANES)
    row = row_iota(shape)
    lane = lane_iota(shape)
    target = jnp.bitwise_and(row + x, 3)
    first = target * 320 + (core * 20 + z * 40)
    inner = jnp.maximum(row - 8, 0)
    step = lax.shift_right_logical(inner, 1)
    odd = inner - 2 * step
    wave = jnp.where(row < 8, first, step)
    quarter = jnp.where(row < 4, 0, jnp.where(row < 8, -1, odd)).astype(F32)
    residue = wave.astype(F32) - 84.0 * floor_div(wave, 84)
    lower = jnp.bitwise_and(wave, 63)
    values = jnp.where(
        lane == 0,
        residue * LOW,
        jnp.where(
            lane == 1,
            (wave - lower).astype(F32),
            jnp.where(
                lane == 2,
                lower.astype(F32),
                jnp.where(lane == 3, quarter * (NLON // 4), 0.0),
            ),
        ),
    )
    return values[:, :16].astype(BF16)


def transform(arrived_ref, c, block_ref, left_ref, table_ref):
    place = lax.axis_index("band")
    factors = wave_factors(place // 16, lax.rem(place // 2, ZS), lax.rem(place, 2))
    lanes8 = lane_iota((8, LANES))
    lanes = lane_iota((16, LANES))
    slot = floor_div(lanes, GROUP)
    band2 = floor_div(lanes.astype(F32) - GROUP * slot, CAP) * 2.0
    step_rows = row_iota((16, LANES)).astype(F32)
    which = row_iota((16, LANES))
    even = jnp.bitwise_and(row_iota((8, LANES)), 1) == 0
    left_ref[c, SHARE * 16 :, :] = jnp.zeros((PARTS * LANES - SHARE * 16, DEPTH), BF16)

    for v in range(TILES):
        columns = slice(LANES * v, LANES * (v + 1))
        messages = [
            arrived_ref[3 * v + s].astype(F32)
            if 3 * v + s < SENDERS
            else jnp.zeros((24, LANES), F32)
            for s in range(3)
        ]
        groups = []
        for s, message in enumerate(messages):
            near = (GROUP * (s - c)) % LANES
            far = (GROUP * (s - 2)) % LANES
            last = pltpu.roll(message[16:24], far, 1)
            groups.append(
                [pltpu.roll(message[8 * t : 8 * t + 8], near, 1) for t in range(3)]
                + [
                    pltpu.roll(message[8 * c : 8 * c + 8], far, 1),
                    pltpu.roll(last, 4, 0) if c else last,
                ]
            )
        for t in range(5):
            block_ref[v, c, t] = jnp.where(
                lanes8 < GROUP,
                groups[0][t],
                jnp.where(
                    lanes8 < 2 * GROUP,
                    groups[1][t],
                    jnp.where(lanes8 < 3 * GROUP, groups[2][t], 0.0),
                ),
            )
        high = jnp.broadcast_to(block_ref[v, c, 4, 2:3, :], (16, LANES))
        low = jnp.broadcast_to(block_ref[v, c, 4, 3:4, :], (16, LANES))
        numbers = jnp.where(
            which == 0, high, jnp.where(which < 3, low, jnp.where(which == 3, 1.0, 0.0))
        ).astype(BF16)
        turns = jnp.dot(factors, numbers, preferred_element_type=F32) * (1.0 / NLON)
        turns = turns - ((turns + MAGIC) - MAGIC)
        square = turns * turns
        series = SIN_TERMS[4]
        for term in SIN_TERMS[3::-1]:
            series = series * square + term
        sine = series * turns
        waves = 1.0 - 2.0 * (sine * sine)
        inner_cosine = waves[8:48]
        inner_sine = jnp.concatenate(
            [
                jnp.where(even, -pltpu.roll(part, 7, 0), pltpu.roll(part, 1, 0))
                for part in (waves[8 + 8 * t : 16 + 8 * t] for t in range(5))
            ],
            axis=0,
        )
        for pair in range(2):
            table_ref[c, 80 * pair : 80 * pair + 80, columns] = jnp.concatenate(
                [
                    waves[d : d + 1] * inner_cosine - waves[4 + d : 5 + d] * inner_sine
                    for d in (2 * pair, 2 * pair + 1)
                ],
                axis=0,
            ).astype(BF16)
        row = band2 + jnp.where(high >= 84.0, 1.0, 0.0)
        mask = jnp.where(row == step_rows, 1.0, 0.0)
        for n in range(SHARE):
            left_ref[c, 16 * n : 16 * n + 16, columns] = (
                mask * block_ref[v, c, n // 8, n % 8 : n % 8 + 1, :]
            ).astype(BF16)


SPANS = ((0, 256), (256, 256), (512, 128))


def transform_own_kernel(own_ref, sum_ref, block_ref, left_ref, table_ref):
    for c in range(CORES):
        transform(own_ref, c, block_ref, left_ref, table_ref)
        for start, size in SPANS:
            sum_ref[c, :, start : start + size] = dot_nt(
                table_ref[c], left_ref[c, start : start + size, :]
            )


def transform_other_kernel(
    other_ref, sum_ref, out0_ref, out1_ref, out2_ref, out3_ref, block_ref, left_ref, table_ref
):
    outs = (out0_ref, out1_ref, out2_ref, out3_ref)
    for c in range(CORES):
        transform(other_ref, c, block_ref, left_ref, table_ref)
        for start, size in SPANS:
            result = sum_ref[c, :, start : start + size] + dot_nt(
                table_ref[c], left_ref[c, start : start + size, :]
            )
            for part in range(size // LANES):
                for k in range(XS):
                    group = (2 * (-k % XS) + c) % GROUPS
                    piece = result[
                        COEFS * k : COEFS * (k + 1), LANES * part : LANES * (part + 1)
                    ]
                    if group:
                        piece = pltpu.roll(piece, 16 * group, 1)
                    outs[k][c, start // LANES + part] = piece.astype(BF16)


def place_kernel(zero_ref, one_ref, two_ref, three_ref, out_hbm, out_ref, semaphores):
    shift = 32 * (lax.axis_index("band") // 16)
    slot = lax.shift_right_logical(lane_iota((COEFS, LANES)), 4)
    sources = (zero_ref, three_ref, two_ref, one_ref)
    copies = []
    for part in range(PARTS):
        values = [sources[g // 2][g % 2, part].astype(F32) for g in range(GROUPS)]
        first = part * TOGETHER
        count = min(TOGETHER, SHARE - first)
        for bit in (4, 2, 1):
            low = jnp.bitwise_and(slot, bit) == 0
            values = [
                jnp.where(low, values[r], values[(r + bit) % TOGETHER]) for r in range(TOGETHER)
            ]
        for q in range(count):
            turn = lax.rem(shift + (LANES - 16 * q), LANES)
            out_ref[first + q] = pltpu.roll(values[-q % TOGETHER], turn, 1).astype(BF16)
        copy = pltpu.make_async_copy(
            out_ref.at[pl.ds(first, count)], out_hbm.at[pl.ds(first, count)], semaphores.at[part]
        )
        copy.start()
        copies.append(copy)
    for copy in copies:
        copy.wait()


def call(kernel, out_shape, scratch=(), limit=32, **keywords):
    return pl.pallas_call(
        kernel,
        out_shape=out_shape,
        scratch_shapes=list(scratch),
        compiler_params=pltpu.CompilerParams(vmem_limit_bytes=limit * 1024 * 1024),
        **keywords,
    )


def x_shift(k):
    return [
        (x * 16 + rest, (x + k) % XS * 16 + rest) for x in range(XS) for rest in range(ZS * CORES)
    ]


def local(jacobian, departures, level_index, level_weight, column_index, record_counts):
    vmem = pl.BlockSpec(memory_space=pltpu.VMEM)
    hbm = pl.BlockSpec(memory_space=pltpu.HBM)
    partial = call(
        contract_kernel,
        jax.ShapeDtypeStruct((KP, RECS), F32),
        [
            pltpu.VMEM((RECS, WIDTH), BF16),
            pltpu.VMEM((CHANNELS, RECS), BF16),
            pltpu.VMEM((RECS, WIDTH), F32),
            pltpu.SemaphoreType.DMA((len(PIECES) + 1,)),
        ],
        limit=53,
        in_specs=[hbm, hbm],
        out_specs=vmem,
    )(jacobian, departures.T)
    others = [
        lax.ppermute(partial, "lev", [(i, (i + k) % 4) for i in range(4)]) for k in (2, 1, 3)
    ]
    place, aux = call(
        prepare_kernel,
        (jax.ShapeDtypeStruct((KL, RECS), F32), jax.ShapeDtypeStruct((8, RECS), F32)),
    )(level_index.T, level_weight.T, column_index.reshape(1, RECS), record_counts.reshape(1, BANDS))
    packed = call(
        pack_kernel,
        jax.ShapeDtypeStruct((SENDERS, 24, LANES), BF16),
        [pltpu.VMEM((KP, RECS), F32)],
    )(partial, *others, place, aux)
    same_core = [
        [x * 16 + z * 2 + c for x in range(XS) for z in range(ZS)] for c in range(CORES)
    ]
    arrived = lax.all_to_all(
        packed, "band", split_axis=0, concat_axis=0, axis_index_groups=same_core, tiled=True
    )
    other = lax.ppermute(arrived, "band", [(i, i ^ 1) for i in range(BANDS)])
    scratch = [
        pltpu.VMEM((TILES, CORES, 5, 8, LANES), F32),
        pltpu.VMEM((CORES, PARTS * LANES, DEPTH), BF16),
        pltpu.VMEM((CORES, XS * COEFS, DEPTH), BF16),
    ]
    own_sum = call(
        transform_own_kernel,
        jax.ShapeDtypeStruct((CORES, XS * COEFS, PARTS * LANES), F32),
        scratch,
    )(arrived)
    spectra = call(
        transform_other_kernel,
        [jax.ShapeDtypeStruct((CORES, PARTS, COEFS, LANES), BF16)] * XS,
        scratch,
    )(other, own_sum)
    received = [spectra[0]] + [None] * 3
    for k in (2, 1, 3):
        received[k] = lax.ppermute(spectra[k], "band", x_shift(k))
    placed = call(
        place_kernel,
        jax.ShapeDtypeStruct((SHARE, COEFS, LANES), BF16),
        [pltpu.VMEM((SHARE, COEFS, LANES), BF16), pltpu.SemaphoreType.DMA((PARTS,))],
        in_specs=[vmem] * 4,
        out_specs=hbm,
    )(*received)
    return jnp.transpose(placed, (0, 2, 1))


def solution(mesh):
    placed = (
        P("band", "lev"),
        P("band", "lev"),
        P("band", None),
        P("band", None),
        P("band"),
        P("band"),
    )
    return jax.shard_map(
        local, mesh=mesh, in_specs=placed, out_specs=P("lev", None, "band"), check_vma=False
    )
```

```python
import functools
import math

import jax
import jax.numpy as jnp
from jax import lax
from jax.experimental import pallas as pl
from jax.experimental.pallas import tpu as pltpu
from jax.sharding import PartitionSpec as P

KL = 54
KP = 56
SHARE = 34
NLON = 2688
ROWS = 2
CAP = 5
CHANNELS = 64
WIDTH = CHANNELS * KL
RECS = 320
PIECES = ((0, 128), (128, 128), (256, 64))
GROUP = 40
GROUPS = 8
XS = 4
ZS = 8
CORES = 2
BANDS = 64
SENDERS = XS * ZS
TILES = 10
LANES = 128
DEPTH = TILES * LANES
COEFS = 40
PARTS = 5
TOGETHER = 8
LOW = 32

F32 = jnp.float32
BF16 = jnp.bfloat16

SIN_TERMS = (
    math.pi,
    -(math.pi**3) / 6.0,
    math.pi**5 / 120.0,
    -(math.pi**7) / 5040.0,
    math.pi**9 / 362880.0,
)
MAGIC = 12582912.0


def dot_nt(a, b):
    return lax.dot_general(a, b, (((1,), (1,)), ((), ())), preferred_element_type=F32)


def dot_tn(a, b):
    return lax.dot_general(a, b, (((0,), (0,)), ((), ())), preferred_element_type=F32)


def lane_iota(shape):
    return lax.broadcasted_iota(jnp.int32, shape, 1)


def row_iota(shape):
    return lax.broadcasted_iota(jnp.int32, shape, 0)


def floor_div(values, divisor):
    return jnp.floor((values.astype(F32) + 0.5) * (1.0 / divisor))


def channel_and_level():
    position = lane_iota((8, WIDTH))
    channel = floor_div(position, KL)
    return channel, position.astype(F32) - KL * channel


def chosen(values, count):
    rows = row_iota((8, values.shape[1]))
    return jnp.concatenate(
        [jnp.where(values == (rows + 8 * t).astype(F32), 1.0, 0.0) for t in range(count // 8)],
        axis=0,
    ).astype(BF16)


def spread_kernel(dep_ref, wide_ref):
    channel, _ = channel_and_level()
    wide_ref[...] = dot_tn(dep_ref[...], chosen(channel, CHANNELS))


def contract_kernel(jac_ref, wide_ref, out_ref):
    _, level = channel_and_level()
    half = WIDTH // 2
    select = chosen(level[:, :half], KP)
    for start, size in PIECES:
        records = slice(start, start + size)
        product = jac_ref[records, :].astype(F32) * wide_ref[records, :]
        product = product[:, :half] + product[:, half:]
        high = product.astype(BF16)
        low = (product - high.astype(F32)).astype(BF16)
        out_ref[:, records] = dot_nt(select, high) + dot_nt(select, low)


def prepare_kernel(index_ref, weight_ref, column_ref, count_ref, place_ref, aux_ref):
    place_ref[...] = index_ref[...].astype(F32) + weight_ref[...].astype(F32)
    lanes = lane_iota((8, RECS))
    band = floor_div(lanes, CAP)
    slot = lanes.astype(F32) - CAP * band
    repeat = jnp.where(
        floor_div(lane_iota((BANDS, RECS)), CAP) == row_iota((BANDS, RECS)).astype(F32),
        1.0,
        0.0,
    ).astype(BF16)
    counts = jnp.broadcast_to(count_ref[...].astype(F32), (8, BANDS)).astype(BF16)
    counts = jnp.dot(counts, repeat, preferred_element_type=F32)
    live = jnp.where(slot < counts, 1.0, 0.0)
    column = jnp.broadcast_to(column_ref[...], (8, RECS)) - band.astype(jnp.int32) * (ROWS * NLON)
    high = lax.shift_right_logical(column, 5)
    low = column - high * LOW
    which = row_iota((8, RECS))
    aux_ref[...] = jnp.where(
        which == 0, live, jnp.where(which == 2, high.astype(F32), low.astype(F32))
    )


def pack_kernel(own_ref, one_ref, two_ref, three_ref, place_ref, aux_ref, out_ref, sum_ref):
    sum_ref[...] = (own_ref[...] + one_ref[...]) + (two_ref[...] + three_ref[...])
    first = lax.axis_index("lev") * SHARE
    live = aux_ref[0:1, :]
    blocks = []
    for start, size in ((0, 24), (24, 8), (32, 8)):
        target = (row_iota((size, RECS)) + (first + start)).astype(F32)
        total = jnp.zeros((size, RECS), F32)
        for k in range(KL):
            hat = jnp.maximum(1.0 - jnp.abs(target - place_ref[k : k + 1, :]), 0.0)
            total = total + hat * sum_ref[k : k + 1, :]
        blocks.append(total * live)
    which = row_iota((8, RECS))
    blocks[2] = jnp.where(which < 2, blocks[2], jnp.where(which < 4, aux_ref[...], 0.0))
    full = 3 * LANES
    upper, middle, last = [
        jnp.concatenate([block, jnp.zeros((block.shape[0], full - RECS), F32)], axis=1)
        for block in blocks
    ]

    def moved(block, source, target):
        return pltpu.roll(block, (target - source) % full, 1)[:, :LANES]

    lanes = lane_iota((24, LANES))
    low_rows = row_iota((8, LANES)) < 4
    for x in range(XS):
        one, two, spot = 2 * GROUP * x, 2 * GROUP * x + GROUP, 2 * GROUP
        rest = jnp.concatenate(
            [
                moved(middle, one, spot),
                moved(middle, two, spot),
                jnp.where(low_rows, moved(last, one, spot), pltpu.roll(moved(last, two, spot), 4, 0)),
            ],
            axis=0,
        )
        message = jnp.where(
            lanes < spot, moved(upper, one, 0), jnp.where(lanes < 3 * GROUP, rest, 0.0)
        ).astype(BF16)
        for z in range(ZS):
            out_ref[x * ZS + z] = message


def wave_factors(x, z, core):
    shape = (48, LANES)
    row = row_iota(shape)
    lane = lane_iota(shape)
    target = jnp.bitwise_and(row + x, 3)
    first = target * 320 + (core * 20 + z * 40)
    inner = jnp.maximum(row - 8, 0)
    step = lax.shift_right_logical(inner, 1)
    odd = inner - 2 * step
    wave = jnp.where(row < 8, first, step)
    quarter = jnp.where(row < 4, 0, jnp.where(row < 8, -1, odd)).astype(F32)
    residue = wave.astype(F32) - 84.0 * floor_div(wave, 84)
    lower = jnp.bitwise_and(wave, 63)
    values = jnp.where(
        lane == 0,
        residue * LOW,
        jnp.where(
            lane == 1,
            (wave - lower).astype(F32),
            jnp.where(
                lane == 2,
                lower.astype(F32),
                jnp.where(lane == 3, quarter * (NLON // 4), 0.0),
            ),
        ),
    )
    return values[:, :16].astype(BF16)


def transform(arrived_ref, c, block_ref, left_ref, table_ref, between=()):
    place = lax.axis_index("band")
    factors = wave_factors(place // 16, lax.rem(place // 2, ZS), lax.rem(place, 2))
    lanes8 = lane_iota((8, LANES))
    lanes = lane_iota((16, LANES))
    step_rows = row_iota((16, LANES)).astype(F32)
    which = row_iota((16, LANES))
    even = jnp.bitwise_and(row_iota((8, LANES)), 1) == 0
    left_ref[SHARE * 16 :, :] = jnp.zeros((PARTS * LANES - SHARE * 16, DEPTH), BF16)

    for v in range(TILES):
        columns = slice(LANES * v, LANES * (v + 1))
        base = LANES * (v % 5)
        block8 = floor_div(lanes8 + base, GROUP)
        block16 = floor_div(lanes + base, GROUP)
        band2 = floor_div((lanes + base).astype(F32) - GROUP * block16, CAP) * 2.0
        total = None
        for e in range(base // GROUP, (base + LANES - 1) // GROUP + 1):
            message = arrived_ref[16 * (v // 5) + e].astype(F32)
            near = (GROUP * (e - c) - base) % LANES
            far = (GROUP * (e - 2) - base) % LANES
            last = pltpu.roll(message[16:24], far, 1)
            parts = [pltpu.roll(message[8 * t : 8 * t + 8], near, 1) for t in range(3)] + [
                pltpu.roll(message[8 * c : 8 * c + 8], far, 1),
                pltpu.roll(last, 4, 0) if c else last,
            ]
            if total is None:
                total = parts
            else:
                total = [jnp.where(block8 == e, new, old) for new, old in zip(parts, total)]
        for t in range(5):
            block_ref[v, t] = total[t]
        high = jnp.broadcast_to(block_ref[v, 4, 2:3, :], (16, LANES))
        low = jnp.broadcast_to(block_ref[v, 4, 3:4, :], (16, LANES))
        numbers = jnp.where(
            which == 0, high, jnp.where(which < 3, low, jnp.where(which == 3, 1.0, 0.0))
        ).astype(BF16)
        turns = jnp.dot(factors, numbers, preferred_element_type=F32) * (1.0 / NLON)
        turns = turns - ((turns + MAGIC) - MAGIC)
        square = turns * turns
        series = SIN_TERMS[4]
        for term in SIN_TERMS[3::-1]:
            series = series * square + term
        sine = series * turns
        waves = 1.0 - 2.0 * (sine * sine)
        inner_cosine = waves[8:48]
        inner_sine = jnp.concatenate(
            [
                jnp.where(even, -pltpu.roll(part, 7, 0), pltpu.roll(part, 1, 0))
                for part in (waves[8 + 8 * t : 16 + 8 * t] for t in range(5))
            ],
            axis=0,
        )
        for pair in range(2):
            table_ref[80 * pair : 80 * pair + 80, columns] = jnp.concatenate(
                [
                    waves[d : d + 1] * inner_cosine - waves[4 + d : 5 + d] * inner_sine
                    for d in (2 * pair, 2 * pair + 1)
                ],
                axis=0,
            ).astype(BF16)
        row = band2 + jnp.where(high >= 84.0, 1.0, 0.0)
        mask = jnp.where(row == step_rows, 1.0, 0.0)
        for n in range(SHARE):
            left_ref[16 * n : 16 * n + 16, columns] = (
                mask * block_ref[v, n // 8, n % 8 : n % 8 + 1, :]
            ).astype(BF16)
        if v % 3 == 2 and v // 3 < len(between):
            between[v // 3]()


SPANS = ((0, 256), (256, 256), (512, 128))


def transform_own_kernel(own_ref, sum_ref, *scratch):
    blocks, lefts, tables = scratch[0:2], scratch[2:4], scratch[4:6]

    def multiply(c, start, size):
        sum_ref[c, :, start : start + size] = dot_nt(
            tables[c][...], lefts[c][start : start + size, :]
        )

    transform(own_ref, 0, blocks[0], lefts[0], tables[0])
    steps = [functools.partial(multiply, 0, *span) for span in SPANS]
    transform(own_ref, 1, blocks[1], lefts[1], tables[1], steps)
    for span in SPANS:
        multiply(1, *span)


def transform_other_kernel(other_ref, sum_ref, out0_ref, out1_ref, out2_ref, out3_ref, *scratch):
    outs = (out0_ref, out1_ref, out2_ref, out3_ref)
    blocks, lefts, tables = scratch[0:2], scratch[2:4], scratch[4:6]

    def multiply(c, start, size):
        result = sum_ref[c, :, start : start + size] + dot_nt(
            tables[c][...], lefts[c][start : start + size, :]
        )
        for part in range(size // LANES):
            for k in range(XS):
                group = (2 * (-k % XS) + c) % GROUPS
                piece = result[COEFS * k : COEFS * (k + 1), LANES * part : LANES * (part + 1)]
                if group:
                    piece = pltpu.roll(piece, 16 * group, 1)
                outs[k][c, start // LANES + part] = piece.astype(BF16)

    transform(other_ref, 0, blocks[0], lefts[0], tables[0])
    steps = [functools.partial(multiply, 0, *span) for span in SPANS]
    transform(other_ref, 1, blocks[1], lefts[1], tables[1], steps)
    for span in SPANS:
        multiply(1, *span)


def place_kernel(zero_ref, one_ref, two_ref, three_ref, out_hbm, out_ref, semaphores):
    shift = 32 * (lax.axis_index("band") // 16)
    slot = lax.shift_right_logical(lane_iota((COEFS, LANES)), 4)
    sources = (zero_ref, three_ref, two_ref, one_ref)
    copies = []
    for part in range(PARTS):
        values = [sources[g // 2][g % 2, part].astype(F32) for g in range(GROUPS)]
        first = part * TOGETHER
        count = min(TOGETHER, SHARE - first)
        for bit in (4, 2, 1):
            low = jnp.bitwise_and(slot, bit) == 0
            values = [
                jnp.where(low, values[r], values[(r + bit) % TOGETHER]) for r in range(TOGETHER)
            ]
        for q in range(count):
            turn = lax.rem(shift + (LANES - 16 * q), LANES)
            out_ref[first + q] = pltpu.roll(values[-q % TOGETHER], turn, 1).astype(BF16)
        copy = pltpu.make_async_copy(
            out_ref.at[pl.ds(first, count)], out_hbm.at[pl.ds(first, count)], semaphores.at[part]
        )
        copy.start()
        copies.append(copy)
    for copy in copies:
        copy.wait()


def call(kernel, out_shape, scratch=(), limit=32, **keywords):
    return pl.pallas_call(
        kernel,
        out_shape=out_shape,
        scratch_shapes=list(scratch),
        compiler_params=pltpu.CompilerParams(vmem_limit_bytes=limit * 1024 * 1024),
        **keywords,
    )


def x_shift(k):
    return [
        (x * 16 + rest, (x + k) % XS * 16 + rest) for x in range(XS) for rest in range(ZS * CORES)
    ]


def local(jacobian, departures, level_index, level_weight, column_index, record_counts):
    vmem = pl.BlockSpec(memory_space=pltpu.VMEM)
    hbm = pl.BlockSpec(memory_space=pltpu.HBM)
    wide = call(spread_kernel, jax.ShapeDtypeStruct((RECS, WIDTH), F32))(departures.T)
    partial = call(contract_kernel, jax.ShapeDtypeStruct((KP, RECS), F32))(jacobian, wide)
    others = [
        lax.ppermute(partial, "lev", [(i, (i + k) % 4) for i in range(4)]) for k in (2, 1, 3)
    ]
    place, aux = call(
        prepare_kernel,
        (jax.ShapeDtypeStruct((KL, RECS), F32), jax.ShapeDtypeStruct((8, RECS), F32)),
    )(level_index.T, level_weight.T, column_index.reshape(1, RECS), record_counts.reshape(1, BANDS))
    packed = call(
        pack_kernel,
        jax.ShapeDtypeStruct((SENDERS, 24, LANES), BF16),
        [pltpu.VMEM((KP, RECS), F32)],
    )(partial, *others, place, aux)
    same_core = [
        [x * 16 + z * 2 + c for x in range(XS) for z in range(ZS)] for c in range(CORES)
    ]
    arrived = lax.all_to_all(
        packed, "band", split_axis=0, concat_axis=0, axis_index_groups=same_core, tiled=True
    )
    other = lax.ppermute(arrived, "band", [(i, i ^ 1) for i in range(BANDS)])
    scratch = (
        [pltpu.VMEM((TILES, 5, 8, LANES), F32)] * CORES
        + [pltpu.VMEM((PARTS * LANES, DEPTH), BF16)] * CORES
        + [pltpu.VMEM((XS * COEFS, DEPTH), BF16)] * CORES
    )
    own_sum = call(
        transform_own_kernel,
        jax.ShapeDtypeStruct((CORES, XS * COEFS, PARTS * LANES), F32),
        scratch,
    )(arrived)
    spectra = call(
        transform_other_kernel,
        [jax.ShapeDtypeStruct((CORES, PARTS, COEFS, LANES), BF16)] * XS,
        scratch,
    )(other, own_sum)
    received = [spectra[0]] + [None] * 3
    for k in (2, 1, 3):
        received[k] = lax.ppermute(spectra[k], "band", x_shift(k))
    placed = call(
        place_kernel,
        jax.ShapeDtypeStruct((SHARE, COEFS, LANES), BF16),
        [pltpu.VMEM((SHARE, COEFS, LANES), BF16), pltpu.SemaphoreType.DMA((PARTS,))],
        in_specs=[vmem] * 4,
        out_specs=hbm,
    )(*received)
    return jnp.transpose(placed, (0, 2, 1))


def solution(mesh):
    placed = (
        P("band", "lev"),
        P("band", "lev"),
        P("band", None),
        P("band", None),
        P("band"),
        P("band"),
    )
    return jax.shard_map(
        local, mesh=mesh, in_specs=placed, out_specs=P("lev", None, "band"), check_vma=False
    )
```

```python
import functools
import math

import jax
import jax.numpy as jnp
from jax import lax
from jax.experimental import pallas as pl
from jax.experimental.pallas import tpu as pltpu
from jax.sharding import PartitionSpec as P

KL = 54
KP = 56
SHARE = 34
ROOM = 40
PACKED = 144
NLON = 2688
ROWS = 2
CAP = 5
CHANNELS = 64
WIDTH = CHANNELS * KL
RECS = 320
PIECES = ((0, 128), (128, 128), (256, 64))
GROUP = 40
GROUPS = 8
XS = 4
ZS = 8
CORES = 2
BANDS = 64
SENDERS = XS * ZS
TILES = 10
LANES = 128
DEPTH = TILES * LANES
COEFS = 40
PARTS = 5
TOGETHER = 8
LOW = 32

F32 = jnp.float32
BF16 = jnp.bfloat16

SIN_TERMS = (
    math.pi,
    -(math.pi**3) / 6.0,
    math.pi**5 / 120.0,
    -(math.pi**7) / 5040.0,
    math.pi**9 / 362880.0,
)
MAGIC = 12582912.0


def dot_nt(a, b):
    return lax.dot_general(a, b, (((1,), (1,)), ((), ())), preferred_element_type=F32)


def dot_tn(a, b):
    return lax.dot_general(a, b, (((0,), (0,)), ((), ())), preferred_element_type=F32)


def lane_iota(shape):
    return lax.broadcasted_iota(jnp.int32, shape, 1)


def row_iota(shape):
    return lax.broadcasted_iota(jnp.int32, shape, 0)


def floor_div(values, divisor):
    return jnp.floor((values.astype(F32) + 0.5) * (1.0 / divisor))


def channel_and_level():
    position = lane_iota((8, WIDTH))
    channel = floor_div(position, KL)
    return channel, position.astype(F32) - KL * channel


def chosen(values, count):
    rows = row_iota((8, values.shape[1]))
    return jnp.concatenate(
        [jnp.where(values == (rows + 8 * t).astype(F32), 1.0, 0.0) for t in range(count // 8)],
        axis=0,
    ).astype(BF16)


def spread_kernel(dep_ref, wide_ref):
    channel, _ = channel_and_level()
    wide_ref[...] = dot_tn(dep_ref[...], chosen(channel, CHANNELS))


def contract_kernel(jac_ref, wide_ref, out_ref):
    _, level = channel_and_level()
    half = WIDTH // 2
    select = chosen(level[:, :half], KP)
    for start, size in PIECES:
        records = slice(start, start + size)
        product = jac_ref[records, :].astype(F32) * wide_ref[records, :]
        product = product[:, :half] + product[:, half:]
        high = product.astype(BF16)
        low = (product - high.astype(F32)).astype(BF16)
        total = dot_nt(select, high) + dot_nt(select, low)
        if size == LANES:
            out_ref[KP * start // LANES : KP * start // LANES + KP, :] = total
        else:
            wide_total = jnp.concatenate([total, jnp.zeros_like(total)], axis=1)
            upper = pltpu.roll(wide_total[32:], size, 1)
            out_ref[2 * KP :, :] = wide_total[:32] + jnp.concatenate(
                [upper, jnp.zeros((8, LANES), F32)], axis=0
            )


def prepare_kernel(index_ref, weight_ref, column_ref, count_ref, hat_ref, aux_ref):
    place = index_ref[...].astype(F32) + weight_ref[...].astype(F32)
    lanes = lane_iota((8, RECS))
    band = floor_div(lanes, CAP)
    slot = lanes.astype(F32) - CAP * band
    repeat = jnp.where(
        floor_div(lane_iota((BANDS, RECS)), CAP) == row_iota((BANDS, RECS)).astype(F32),
        1.0,
        0.0,
    ).astype(BF16)
    counts = jnp.broadcast_to(count_ref[...].astype(F32), (8, BANDS)).astype(BF16)
    counts = jnp.dot(counts, repeat, preferred_element_type=F32)
    live = jnp.where(slot < counts, 1.0, 0.0)
    column = jnp.broadcast_to(column_ref[...], (8, RECS)) - band.astype(jnp.int32) * (ROWS * NLON)
    high = lax.shift_right_logical(column, 5)
    low = column - high * LOW
    which = row_iota((8, RECS))
    aux_ref[...] = jnp.where(which == 2, high.astype(F32), low.astype(F32))
    first = lax.axis_index("lev") * SHARE
    target = (row_iota((ROOM, RECS)) + first).astype(F32)
    for k in range(KL):
        hat_ref[k] = jnp.maximum(1.0 - jnp.abs(target - place[k : k + 1, :]), 0.0) * live[0:1, :]


def pack_kernel(own_ref, one_ref, two_ref, three_ref, hat_ref, aux_ref, out_ref, sum_ref):
    total = (own_ref[...] + one_ref[...]) + (two_ref[...] + three_ref[...])
    sum_ref[:, 0:LANES] = total[0:KP]
    sum_ref[:, LANES : 2 * LANES] = total[KP : 2 * KP]
    sum_ref[0:32, 2 * LANES :] = total[2 * KP :]
    sum_ref[32:, 2 * LANES :] = pltpu.roll(total[2 * KP : 2 * KP + 24], 64, 1)
    profile = jnp.zeros((ROOM, RECS), F32)
    for k in range(KL):
        profile = profile + hat_ref[k] * sum_ref[k : k + 1, 0:RECS]
    blocks = [profile[0:24], profile[24:32], profile[32:40]]
    which = row_iota((8, RECS))
    blocks[2] = jnp.where(which < 2, blocks[2], jnp.where(which < 4, aux_ref[...], 0.0))
    full = 3 * LANES
    upper, middle, last = [
        jnp.concatenate([block, jnp.zeros((block.shape[0], full - RECS), F32)], axis=1)
        for block in blocks
    ]

    def moved(block, source, target):
        return pltpu.roll(block, (target - source) % full, 1)[:, :LANES]

    lanes = lane_iota((24, LANES))
    low_rows = row_iota((8, LANES)) < 4
    for x in range(XS):
        one, two, spot = 2 * GROUP * x, 2 * GROUP * x + GROUP, 2 * GROUP
        rest = jnp.concatenate(
            [
                moved(middle, one, spot),
                moved(middle, two, spot),
                jnp.where(low_rows, moved(last, one, spot), pltpu.roll(moved(last, two, spot), 4, 0)),
            ],
            axis=0,
        )
        message = jnp.where(
            lanes < spot, moved(upper, one, 0), jnp.where(lanes < 3 * GROUP, rest, 0.0)
        ).astype(BF16)
        for z in range(ZS):
            out_ref[x * ZS + z] = message


def wave_factors(x, z, core):
    shape = (48, LANES)
    row = row_iota(shape)
    lane = lane_iota(shape)
    target = jnp.bitwise_and(row + x, 3)
    first = target * 320 + (core * 20 + z * 40)
    inner = jnp.maximum(row - 8, 0)
    step = lax.shift_right_logical(inner, 1)
    odd = inner - 2 * step
    wave = jnp.where(row < 8, first, step)
    quarter = jnp.where(row < 4, 0, jnp.where(row < 8, -1, odd)).astype(F32)
    residue = wave.astype(F32) - 84.0 * floor_div(wave, 84)
    lower = jnp.bitwise_and(wave, 63)
    values = jnp.where(
        lane == 0,
        residue * LOW,
        jnp.where(
            lane == 1,
            (wave - lower).astype(F32),
            jnp.where(
                lane == 2,
                lower.astype(F32),
                jnp.where(lane == 3, quarter * (NLON // 4), 0.0),
            ),
        ),
    )
    return values[:, :16].astype(BF16)


def transform(arrived_ref, c, block_ref, left_ref, table_ref, between=()):
    place = lax.axis_index("band")
    factors = wave_factors(place // 16, lax.rem(place // 2, ZS), lax.rem(place, 2))
    lanes8 = lane_iota((8, LANES))
    lanes = lane_iota((16, LANES))
    step_rows = row_iota((16, LANES)).astype(F32)
    which = row_iota((16, LANES))
    even = jnp.bitwise_and(row_iota((8, LANES)), 1) == 0
    left_ref[SHARE * 16 :, :] = jnp.zeros((PARTS * LANES - SHARE * 16, DEPTH), BF16)

    for v in range(TILES):
        columns = slice(LANES * v, LANES * (v + 1))
        base = LANES * (v % 5)
        block8 = floor_div(lanes8 + base, GROUP)
        block16 = floor_div(lanes + base, GROUP)
        band2 = floor_div((lanes + base).astype(F32) - GROUP * block16, CAP) * 2.0
        total = None
        for e in range(base // GROUP, (base + LANES - 1) // GROUP + 1):
            message = arrived_ref[16 * (v // 5) + e].astype(F32)
            near = (GROUP * (e - c) - base) % LANES
            far = (GROUP * (e - 2) - base) % LANES
            last = pltpu.roll(message[16:24], far, 1)
            parts = [pltpu.roll(message[8 * t : 8 * t + 8], near, 1) for t in range(3)] + [
                pltpu.roll(message[8 * c : 8 * c + 8], far, 1),
                pltpu.roll(last, 4, 0) if c else last,
            ]
            if total is None:
                total = parts
            else:
                total = [jnp.where(block8 == e, new, old) for new, old in zip(parts, total)]
        for t in range(5):
            block_ref[v, t] = total[t]
        high = jnp.broadcast_to(block_ref[v, 4, 2:3, :], (16, LANES))
        low = jnp.broadcast_to(block_ref[v, 4, 3:4, :], (16, LANES))
        numbers = jnp.where(
            which == 0, high, jnp.where(which < 3, low, jnp.where(which == 3, 1.0, 0.0))
        ).astype(BF16)
        turns = jnp.dot(factors, numbers, preferred_element_type=F32) * (1.0 / NLON)
        turns = turns - ((turns + MAGIC) - MAGIC)
        square = turns * turns
        series = SIN_TERMS[4]
        for term in SIN_TERMS[3::-1]:
            series = series * square + term
        sine = series * turns
        waves = 1.0 - 2.0 * (sine * sine)
        inner_cosine = waves[8:48]
        inner_sine = jnp.concatenate(
            [
                jnp.where(even, -pltpu.roll(part, 7, 0), pltpu.roll(part, 1, 0))
                for part in (waves[8 + 8 * t : 16 + 8 * t] for t in range(5))
            ],
            axis=0,
        )
        for pair in range(2):
            table_ref[80 * pair : 80 * pair + 80, columns] = jnp.concatenate(
                [
                    waves[d : d + 1] * inner_cosine - waves[4 + d : 5 + d] * inner_sine
                    for d in (2 * pair, 2 * pair + 1)
                ],
                axis=0,
            ).astype(BF16)
        row = band2 + jnp.where(high >= 84.0, 1.0, 0.0)
        mask = jnp.where(row == step_rows, 1.0, 0.0)
        for n in range(SHARE):
            left_ref[16 * n : 16 * n + 16, columns] = (
                mask * block_ref[v, n // 8, n % 8 : n % 8 + 1, :]
            ).astype(BF16)
        if v % 3 == 2 and v // 3 < len(between):
            between[v // 3]()


SPANS = ((0, 256), (256, 256), (512, 128))


def transform_own_kernel(own_ref, sum_ref, *scratch):
    blocks, lefts, tables = scratch[0:2], scratch[2:4], scratch[4:6]

    def multiply(c, start, size):
        sum_ref[c, :, start : start + size] = dot_nt(
            tables[c][...], lefts[c][start : start + size, :]
        )

    transform(own_ref, 0, blocks[0], lefts[0], tables[0])
    steps = [functools.partial(multiply, 0, *span) for span in SPANS]
    transform(own_ref, 1, blocks[1], lefts[1], tables[1], steps)
    for span in SPANS:
        multiply(1, *span)


def transform_other_kernel(other_ref, sum_ref, out0_ref, out1_ref, out2_ref, out3_ref, *scratch):
    outs = (out0_ref, out1_ref, out2_ref, out3_ref)
    blocks, lefts, tables = scratch[0:2], scratch[2:4], scratch[4:6]

    def multiply(c, start, size):
        result = sum_ref[c, :, start : start + size] + dot_nt(
            tables[c][...], lefts[c][start : start + size, :]
        )
        for part in range(size // LANES):
            for k in range(XS):
                group = (2 * (-k % XS) + c) % GROUPS
                piece = result[COEFS * k : COEFS * (k + 1), LANES * part : LANES * (part + 1)]
                if group:
                    piece = pltpu.roll(piece, 16 * group, 1)
                outs[k][c, start // LANES + part] = piece.astype(BF16)

    transform(other_ref, 0, blocks[0], lefts[0], tables[0])
    steps = [functools.partial(multiply, 0, *span) for span in SPANS]
    transform(other_ref, 1, blocks[1], lefts[1], tables[1], steps)
    for span in SPANS:
        multiply(1, *span)


def place_kernel(zero_ref, one_ref, two_ref, three_ref, out_hbm, out_ref, semaphores):
    shift = 32 * (lax.axis_index("band") // 16)
    slot = lax.shift_right_logical(lane_iota((COEFS, LANES)), 4)
    sources = (zero_ref, three_ref, two_ref, one_ref)
    copies = []
    for part in range(PARTS):
        values = [sources[g // 2][g % 2, part].astype(F32) for g in range(GROUPS)]
        first = part * TOGETHER
        count = min(TOGETHER, SHARE - first)
        for bit in (4, 2, 1):
            low = jnp.bitwise_and(slot, bit) == 0
            values = [
                jnp.where(low, values[r], values[(r + bit) % TOGETHER]) for r in range(TOGETHER)
            ]
        for q in range(count):
            turn = lax.rem(shift + (LANES - 16 * q), LANES)
            out_ref[first + q] = pltpu.roll(values[-q % TOGETHER], turn, 1).astype(BF16)
        copy = pltpu.make_async_copy(
            out_ref.at[pl.ds(first, count)], out_hbm.at[pl.ds(first, count)], semaphores.at[part]
        )
        copy.start()
        copies.append(copy)
    for copy in copies:
        copy.wait()


def call(kernel, out_shape, scratch=(), limit=32, **keywords):
    return pl.pallas_call(
        kernel,
        out_shape=out_shape,
        scratch_shapes=list(scratch),
        compiler_params=pltpu.CompilerParams(vmem_limit_bytes=limit * 1024 * 1024),
        **keywords,
    )


def x_shift(k):
    return [
        (x * 16 + rest, (x + k) % XS * 16 + rest) for x in range(XS) for rest in range(ZS * CORES)
    ]


def local(jacobian, departures, level_index, level_weight, column_index, record_counts):
    vmem = pl.BlockSpec(memory_space=pltpu.VMEM)
    hbm = pl.BlockSpec(memory_space=pltpu.HBM)
    wide = call(spread_kernel, jax.ShapeDtypeStruct((RECS, WIDTH), F32))(departures.T)
    partial = call(contract_kernel, jax.ShapeDtypeStruct((PACKED, LANES), F32))(jacobian, wide)
    others = [
        lax.ppermute(partial, "lev", [(i, (i + k) % 4) for i in range(4)]) for k in (2, 1, 3)
    ]
    hat, aux = call(
        prepare_kernel,
        (jax.ShapeDtypeStruct((KL, ROOM, RECS), F32), jax.ShapeDtypeStruct((8, RECS), F32)),
    )(level_index.T, level_weight.T, column_index.reshape(1, RECS), record_counts.reshape(1, BANDS))
    packed = call(
        pack_kernel,
        jax.ShapeDtypeStruct((SENDERS, 24, LANES), BF16),
        [pltpu.VMEM((KP, 3 * LANES), F32)],
    )(partial, *others, hat, aux)
    same_core = [
        [x * 16 + z * 2 + c for x in range(XS) for z in range(ZS)] for c in range(CORES)
    ]
    arrived = lax.all_to_all(
        packed, "band", split_axis=0, concat_axis=0, axis_index_groups=same_core, tiled=True
    )
    other = lax.ppermute(arrived, "band", [(i, i ^ 1) for i in range(BANDS)])
    scratch = (
        [pltpu.VMEM((TILES, 5, 8, LANES), F32)] * CORES
        + [pltpu.VMEM((PARTS * LANES, DEPTH), BF16)] * CORES
        + [pltpu.VMEM((XS * COEFS, DEPTH), BF16)] * CORES
    )
    own_sum = call(
        transform_own_kernel,
        jax.ShapeDtypeStruct((CORES, XS * COEFS, PARTS * LANES), F32),
        scratch,
    )(arrived)
    spectra = call(
        transform_other_kernel,
        [jax.ShapeDtypeStruct((CORES, PARTS, COEFS, LANES), BF16)] * XS,
        scratch,
    )(other, own_sum)
    received = [spectra[0]] + [None] * 3
    for k in (2, 1, 3):
        received[k] = lax.ppermute(spectra[k], "band", x_shift(k))
    placed = call(
        place_kernel,
        jax.ShapeDtypeStruct((SHARE, COEFS, LANES), BF16),
        [pltpu.VMEM((SHARE, COEFS, LANES), BF16), pltpu.SemaphoreType.DMA((PARTS,))],
        in_specs=[vmem] * 4,
        out_specs=hbm,
    )(*received)
    return jnp.transpose(placed, (0, 2, 1))


def solution(mesh):
    placed = (
        P("band", "lev"),
        P("band", "lev"),
        P("band", None),
        P("band", None),
        P("band"),
        P("band"),
    )
    return jax.shard_map(
        local, mesh=mesh, in_specs=placed, out_specs=P("lev", None, "band"), check_vma=False
    )
```

```python
import functools
import math

import jax
import jax.numpy as jnp
from jax import lax
from jax.experimental import pallas as pl
from jax.experimental.pallas import tpu as pltpu
from jax.sharding import PartitionSpec as P

KL = 54
KP = 56
SHARE = 34
ROOM = 40
PACKED = 144
NLON = 2688
ROWS = 2
CAP = 5
CHANNELS = 64
WIDTH = CHANNELS * KL
RECS = 320
PIECES = ((0, 128), (128, 128), (256, 64))
GROUP = 40
GROUPS = 8
XS = 4
ZS = 8
CORES = 2
BANDS = 64
SENDERS = XS * ZS
TILES = 10
LANES = 128
DEPTH = TILES * LANES
COEFS = 40
PARTS = 5
TOGETHER = 8
LOW = 32

F32 = jnp.float32
BF16 = jnp.bfloat16

SIN_TERMS = (
    math.pi,
    -(math.pi**3) / 6.0,
    math.pi**5 / 120.0,
    -(math.pi**7) / 5040.0,
    math.pi**9 / 362880.0,
)
MAGIC = 12582912.0


def dot_nt(a, b):
    return lax.dot_general(a, b, (((1,), (1,)), ((), ())), preferred_element_type=F32)


def dot_tn(a, b):
    return lax.dot_general(a, b, (((0,), (0,)), ((), ())), preferred_element_type=F32)


def lane_iota(shape):
    return lax.broadcasted_iota(jnp.int32, shape, 1)


def row_iota(shape):
    return lax.broadcasted_iota(jnp.int32, shape, 0)


def floor_div(values, divisor):
    return jnp.floor((values.astype(F32) + 0.5) * (1.0 / divisor))


def channel_and_level():
    position = lane_iota((8, WIDTH))
    channel = floor_div(position, KL)
    return channel, position.astype(F32) - KL * channel


def chosen(values, count):
    rows = row_iota((8, values.shape[1]))
    return jnp.concatenate(
        [jnp.where(values == (rows + 8 * t).astype(F32), 1.0, 0.0) for t in range(count // 8)],
        axis=0,
    ).astype(BF16)


def spread_kernel(dep_ref, wide_ref):
    channel, _ = channel_and_level()
    wide_ref[...] = dot_tn(dep_ref[...], chosen(channel, CHANNELS))


def contract_kernel(jac_ref, wide_ref, out_ref):
    _, level = channel_and_level()
    half = WIDTH // 2
    select = chosen(level[:, :half], KP)
    for start, size in PIECES:
        records = slice(start, start + size)
        product = jac_ref[records, :].astype(F32) * wide_ref[records, :]
        product = product[:, :half] + product[:, half:]
        high = product.astype(BF16)
        low = (product - high.astype(F32)).astype(BF16)
        total = dot_nt(select, high) + dot_nt(select, low)
        if size == LANES:
            out_ref[KP * start // LANES : KP * start // LANES + KP, :] = total
        else:
            wide_total = jnp.concatenate([total, jnp.zeros_like(total)], axis=1)
            upper = pltpu.roll(wide_total[32:], size, 1)
            out_ref[2 * KP :, :] = wide_total[:32] + jnp.concatenate(
                [upper, jnp.zeros((8, LANES), F32)], axis=0
            )


def prepare_kernel(index_ref, weight_ref, column_ref, count_ref, hat_ref, aux_ref):
    place = index_ref[...].astype(F32) + weight_ref[...].astype(F32)
    lanes = lane_iota((8, RECS))
    band = floor_div(lanes, CAP)
    slot = lanes.astype(F32) - CAP * band
    repeat = jnp.where(
        floor_div(lane_iota((BANDS, RECS)), CAP) == row_iota((BANDS, RECS)).astype(F32),
        1.0,
        0.0,
    ).astype(BF16)
    counts = jnp.broadcast_to(count_ref[...].astype(F32), (8, BANDS)).astype(BF16)
    counts = jnp.dot(counts, repeat, preferred_element_type=F32)
    live = jnp.where(slot < counts, 1.0, 0.0)
    column = jnp.broadcast_to(column_ref[...], (8, RECS)) - band.astype(jnp.int32) * (ROWS * NLON)
    high = lax.shift_right_logical(column, 5)
    low = column - high * LOW
    which = row_iota((8, RECS))
    aux_ref[...] = jnp.where(which == 2, high.astype(F32), low.astype(F32))
    first = lax.axis_index("lev") * SHARE
    target = (row_iota((ROOM, RECS)) + first).astype(F32)
    for k in range(KL):
        hat_ref[k] = jnp.maximum(1.0 - jnp.abs(target - place[k : k + 1, :]), 0.0) * live[0:1, :]


def pack_kernel(own_ref, one_ref, two_ref, three_ref, hat_ref, aux_ref, out_ref, sum_ref):
    total = (own_ref[...] + one_ref[...]) + (two_ref[...] + three_ref[...])
    sum_ref[:, 0:LANES] = total[0:KP]
    sum_ref[:, LANES : 2 * LANES] = total[KP : 2 * KP]
    sum_ref[0:32, 2 * LANES :] = total[2 * KP :]
    sum_ref[32:, 2 * LANES :] = pltpu.roll(total[2 * KP : 2 * KP + 24], 64, 1)
    profile = jnp.zeros((ROOM, RECS), F32)
    for k in range(KL):
        profile = profile + hat_ref[k] * sum_ref[k : k + 1, 0:RECS]
    blocks = [profile[0:24], profile[24:32], profile[32:40]]
    which = row_iota((8, RECS))
    blocks[2] = jnp.where(which < 2, blocks[2], jnp.where(which < 4, aux_ref[...], 0.0))
    full = 3 * LANES
    upper, middle, last = [
        jnp.concatenate([block, jnp.zeros((block.shape[0], full - RECS), F32)], axis=1)
        for block in blocks
    ]

    def moved(block, source, target):
        return pltpu.roll(block, (target - source) % full, 1)[:, :LANES]

    lanes = lane_iota((24, LANES))
    low_rows = row_iota((8, LANES)) < 4
    for x in range(XS):
        one, two, spot = 2 * GROUP * x, 2 * GROUP * x + GROUP, 2 * GROUP
        rest = jnp.concatenate(
            [
                moved(middle, one, spot),
                moved(middle, two, spot),
                jnp.where(low_rows, moved(last, one, spot), pltpu.roll(moved(last, two, spot), 4, 0)),
            ],
            axis=0,
        )
        message = jnp.where(
            lanes < spot, moved(upper, one, 0), jnp.where(lanes < 3 * GROUP, rest, 0.0)
        ).astype(BF16)
        for z in range(ZS):
            out_ref[x * ZS + z] = message


def wave_factors(x, z, core):
    shape = (48, LANES)
    row = row_iota(shape)
    lane = lane_iota(shape)
    target = jnp.bitwise_and(row + x, 3)
    first = target * 320 + (core * 20 + z * 40)
    inner = jnp.maximum(row - 8, 0)
    step = lax.shift_right_logical(inner, 1)
    odd = inner - 2 * step
    wave = jnp.where(row < 8, first, step)
    quarter = jnp.where(row < 4, 0, jnp.where(row < 8, -1, odd)).astype(F32)
    residue = wave.astype(F32) - 84.0 * floor_div(wave, 84)
    lower = jnp.bitwise_and(wave, 63)
    values = jnp.where(
        lane == 0,
        residue * LOW,
        jnp.where(
            lane == 1,
            (wave - lower).astype(F32),
            jnp.where(
                lane == 2,
                lower.astype(F32),
                jnp.where(lane == 3, quarter * (NLON // 4), 0.0),
            ),
        ),
    )
    return values[:, :16].astype(BF16)


def transform(arrived_ref, c, block_ref, left_ref, table_ref, between=()):
    place = lax.axis_index("band")
    factors = wave_factors(place // 16, lax.rem(place // 2, ZS), lax.rem(place, 2))
    lanes8 = lane_iota((8, LANES))
    lanes = lane_iota((16, LANES))
    step_rows = row_iota((16, LANES)).astype(F32)
    which = row_iota((16, LANES))
    even = jnp.bitwise_and(row_iota((8, LANES)), 1) == 0

    for v in range(TILES):
        columns = slice(LANES * v, LANES * (v + 1))
        base = LANES * (v % 5)
        block8 = floor_div(lanes8 + base, GROUP)
        block16 = floor_div(lanes + base, GROUP)
        band2 = floor_div((lanes + base).astype(F32) - GROUP * block16, CAP) * 2.0
        total = None
        for e in range(base // GROUP, (base + LANES - 1) // GROUP + 1):
            message = arrived_ref[16 * (v // 5) + e].astype(F32)
            near = (GROUP * (e - c) - base) % LANES
            far = (GROUP * (e - 2) - base) % LANES
            last = pltpu.roll(message[16:24], far, 1)
            parts = [pltpu.roll(message[8 * t : 8 * t + 8], near, 1) for t in range(3)] + [
                pltpu.roll(message[8 * c : 8 * c + 8], far, 1),
                pltpu.roll(last, 4, 0) if c else last,
            ]
            if total is None:
                total = parts
            else:
                total = [jnp.where(block8 == e, new, old) for new, old in zip(parts, total)]
        for t in range(5):
            block_ref[v, t] = total[t]
        high = jnp.broadcast_to(block_ref[v, 4, 2:3, :], (16, LANES))
        low = jnp.broadcast_to(block_ref[v, 4, 3:4, :], (16, LANES))
        numbers = jnp.where(
            which == 0, high, jnp.where(which < 3, low, jnp.where(which == 3, 1.0, 0.0))
        ).astype(BF16)
        turns = jnp.dot(factors, numbers, preferred_element_type=F32) * (1.0 / NLON)
        turns = turns - ((turns + MAGIC) - MAGIC)
        square = turns * turns
        series = SIN_TERMS[4]
        for term in SIN_TERMS[3::-1]:
            series = series * square + term
        sine = series * turns
        waves = 1.0 - 2.0 * (sine * sine)
        inner_cosine = waves[8:48]
        inner_sine = jnp.concatenate(
            [
                jnp.where(even, -pltpu.roll(part, 7, 0), pltpu.roll(part, 1, 0))
                for part in (waves[8 + 8 * t : 16 + 8 * t] for t in range(5))
            ],
            axis=0,
        )
        for pair in range(2):
            table_ref[80 * pair : 80 * pair + 80, columns] = jnp.concatenate(
                [
                    waves[d : d + 1] * inner_cosine - waves[4 + d : 5 + d] * inner_sine
                    for d in (2 * pair, 2 * pair + 1)
                ],
                axis=0,
            ).astype(BF16)
        row = band2 + jnp.where(high >= 84.0, 1.0, 0.0)
        mask = jnp.where(row == step_rows, 1.0, 0.0)
        for n in range(SHARE):
            left_ref[16 * n : 16 * n + 16, columns] = (
                mask * block_ref[v, n // 8, n % 8 : n % 8 + 1, :]
            ).astype(BF16)
        if v % 3 == 2 and v // 3 < len(between):
            between[v // 3]()


SPANS = ((0, 256), (256, 256), (512, 32))


def transform_own_kernel(own_ref, sum_ref, *scratch):
    blocks, lefts, tables = scratch[0:2], scratch[2:4], scratch[4:6]

    def multiply(c, start, size):
        sum_ref[c, :, start : start + size] = dot_nt(
            tables[c][...], lefts[c][start : start + size, :]
        )

    transform(own_ref, 0, blocks[0], lefts[0], tables[0])
    steps = [functools.partial(multiply, 0, *span) for span in SPANS]
    transform(own_ref, 1, blocks[1], lefts[1], tables[1], steps)
    for span in SPANS:
        multiply(1, *span)


def transform_other_kernel(other_ref, sum_ref, out0_ref, out1_ref, out2_ref, out3_ref, *scratch):
    outs = (out0_ref, out1_ref, out2_ref, out3_ref)
    blocks, lefts, tables = scratch[0:2], scratch[2:4], scratch[4:6]

    short = {}

    def turned(result, c, k):
        group = (2 * (-k % XS) + c) % GROUPS
        piece = result[COEFS * k : COEFS * (k + 1)]
        return pltpu.roll(piece, 16 * group, 1) if group else piece

    def multiply(c, start, size):
        result = sum_ref[c, :, start : start + size] + dot_nt(
            tables[c][...], lefts[c][start : start + size, :]
        )
        for part in range(size // LANES):
            for k in range(XS):
                outs[k][4 * c + start // LANES + part] = turned(
                    result[:, LANES * part : LANES * (part + 1)], c, k
                ).astype(BF16)
        if size < LANES:
            short[c] = jnp.concatenate(
                [result, jnp.zeros((XS * COEFS, LANES - size), F32)], axis=1
            )
            if len(short) == CORES:
                for k in range(XS):
                    outs[k][8] = (
                        turned(short[0], 0, k) + pltpu.roll(turned(short[1], 1, k), 64, 1)
                    ).astype(BF16)

    transform(other_ref, 0, blocks[0], lefts[0], tables[0])
    steps = [functools.partial(multiply, 0, *span) for span in SPANS]
    transform(other_ref, 1, blocks[1], lefts[1], tables[1], steps)
    for span in SPANS:
        multiply(1, *span)


def place_kernel(zero_ref, one_ref, two_ref, three_ref, out_hbm, out_ref, semaphores):
    shift = 32 * (lax.axis_index("band") // 16)
    slot = lax.shift_right_logical(lane_iota((COEFS, LANES)), 4)
    sources = (zero_ref, three_ref, two_ref, one_ref)
    copies = []
    for part in range(PARTS):
        values = [
            sources[g // 2][4 * (g % 2) + part if part < 4 else 8].astype(F32)
            for g in range(GROUPS)
        ]
        if part == 4:
            values = [pltpu.roll(v, 64, 1) if g % 2 else v for g, v in enumerate(values)]
        first = part * TOGETHER
        count = min(TOGETHER, SHARE - first)
        for bit in (4, 2, 1):
            low = jnp.bitwise_and(slot, bit) == 0
            values = [
                jnp.where(low, values[r], values[(r + bit) % TOGETHER]) for r in range(TOGETHER)
            ]
        for q in range(count):
            turn = lax.rem(shift + (LANES - 16 * q), LANES)
            out_ref[first + q] = pltpu.roll(values[-q % TOGETHER], turn, 1).astype(BF16)
        copy = pltpu.make_async_copy(
            out_ref.at[pl.ds(first, count)], out_hbm.at[pl.ds(first, count)], semaphores.at[part]
        )
        copy.start()
        copies.append(copy)
    for copy in copies:
        copy.wait()


def call(kernel, out_shape, scratch=(), limit=32, **keywords):
    return pl.pallas_call(
        kernel,
        out_shape=out_shape,
        scratch_shapes=list(scratch),
        compiler_params=pltpu.CompilerParams(vmem_limit_bytes=limit * 1024 * 1024),
        **keywords,
    )


def x_shift(k):
    return [
        (x * 16 + rest, (x + k) % XS * 16 + rest) for x in range(XS) for rest in range(ZS * CORES)
    ]


def local(jacobian, departures, level_index, level_weight, column_index, record_counts):
    vmem = pl.BlockSpec(memory_space=pltpu.VMEM)
    hbm = pl.BlockSpec(memory_space=pltpu.HBM)
    wide = call(spread_kernel, jax.ShapeDtypeStruct((RECS, WIDTH), F32))(departures.T)
    partial = call(contract_kernel, jax.ShapeDtypeStruct((PACKED, LANES), F32))(jacobian, wide)
    others = [
        lax.ppermute(partial, "lev", [(i, (i + k) % 4) for i in range(4)]) for k in (2, 1, 3)
    ]
    hat, aux = call(
        prepare_kernel,
        (jax.ShapeDtypeStruct((KL, ROOM, RECS), F32), jax.ShapeDtypeStruct((8, RECS), F32)),
    )(level_index.T, level_weight.T, column_index.reshape(1, RECS), record_counts.reshape(1, BANDS))
    packed = call(
        pack_kernel,
        jax.ShapeDtypeStruct((SENDERS, 24, LANES), BF16),
        [pltpu.VMEM((KP, 3 * LANES), F32)],
    )(partial, *others, hat, aux)
    same_core = [
        [x * 16 + z * 2 + c for x in range(XS) for z in range(ZS)] for c in range(CORES)
    ]
    arrived = lax.all_to_all(
        packed, "band", split_axis=0, concat_axis=0, axis_index_groups=same_core, tiled=True
    )
    other = lax.ppermute(arrived, "band", [(i, i ^ 1) for i in range(BANDS)])
    scratch = (
        [pltpu.VMEM((TILES, 5, 8, LANES), F32)] * CORES
        + [pltpu.VMEM((SHARE * 16, DEPTH), BF16)] * CORES
        + [pltpu.VMEM((XS * COEFS, DEPTH), BF16)] * CORES
    )
    own_sum = call(
        transform_own_kernel,
        jax.ShapeDtypeStruct((CORES, XS * COEFS, PARTS * LANES), F32),
        scratch,
    )(arrived)
    spectra = call(
        transform_other_kernel,
        [jax.ShapeDtypeStruct((9, COEFS, LANES), BF16)] * XS,
        scratch,
    )(other, own_sum)
    received = [spectra[0]] + [None] * 3
    for k in (2, 1, 3):
        received[k] = lax.ppermute(spectra[k], "band", x_shift(k))
    placed = call(
        place_kernel,
        jax.ShapeDtypeStruct((SHARE, COEFS, LANES), BF16),
        [pltpu.VMEM((SHARE, COEFS, LANES), BF16), pltpu.SemaphoreType.DMA((PARTS,))],
        in_specs=[vmem] * 4,
        out_specs=hbm,
    )(*received)
    return jnp.transpose(placed, (0, 2, 1))


def solution(mesh):
    placed = (
        P("band", "lev"),
        P("band", "lev"),
        P("band", None),
        P("band", None),
        P("band"),
        P("band"),
    )
    return jax.shard_map(
        local, mesh=mesh, in_specs=placed, out_specs=P("lev", None, "band"), check_vma=False
    )
```
